128 devices in a mesh: visit: 16 (over z, y_lo, core), grp: 8 (over x, y_hi).
Axes of the slice: x: 4, y: 4 (y_hi: 2, y_lo: 2; y = y_hi * 2 + y_lo), z: 4, core: 2. Of those that a mesh axis runs over, the one named last changes fastest.
Arguments:
- coadd_tiles: float32 [4096, 16384], P('visit', 'grp'), may hold values from -9 to 9
- science: float32 [4096, 16384], P('visit', 'grp'), may hold values from -16 to 16
- correlation: int32 [16], P('visit'), may hold values from 0 to 15, as said below
- offset: int32 [16], P('visit'), may hold values from 10 to 246
Outputs:
- difference: float32 [4096, 16384], P('visit', 'grp')
- significance: float32 [4096, 16384], P('visit', 'grp')
- match_coef: float32 [16, 6], P('visit')
The draws below stay inside these ranges and needn't reach their ends.
Inputs may be any that keep to these rules, and one draw needn't show every extreme that they name: correlation is a permutation of 0 .. 15.
All inputs are finite; a program needn't handle non-finite values.
Results may differ from the reference program's by a relative error of at most 0.0003.
Values sent between devices are 32-bit elements; how exact they have to be, the bound alone decides.
No kernel may reach another device: no remote copies, remote signals or barrier semaphores. Data moves between devices by JAX's collectives and lax.ppermute only.
A program may use at most 128 MiB of HBM per device.

```python
import jax
import jax.numpy as jnp
from jax import lax

ROWS = 256
COLS = 2048
KER_HALF = 10
BASIS = 5
FILT_HALF = 6
N_VISIT = 16
N_GRP = 8


def sky_tiles(key):
    layout = (N_VISIT * ROWS, N_GRP * COLS)
    values = jax.random.truncated_normal(jax.random.fold_in(key, 11), -5.0, 5.0, layout, jnp.float32)
    stripe = (jnp.arange(N_GRP * COLS) // COLS).astype(jnp.float32)
    amplitude = 3.0 ** (0.5 * stripe / max(N_GRP - 1, 1))
    return values * amplitude[None, :]


def sky_table(key):
    ordering = jax.random.permutation(jax.random.fold_in(key, 12), N_VISIT).astype(jnp.int32)
    shifts = jax.random.randint(jax.random.fold_in(key, 13), (N_VISIT,), KER_HALF, ROWS - KER_HALF + 1).astype(jnp.int32)
    chosen = jax.random.permutation(jax.random.fold_in(key, 18), N_VISIT).astype(jnp.int32)
    shifts = shifts.at[chosen[0]].set(ROWS - KER_HALF)
    shifts = shifts.at[chosen[1]].set(KER_HALF)
    return (ordering, shifts.astype(jnp.int32))


def draw_coadd_tiles(key, part):
    return sky_tiles(key)


def draw_correlation(key, part):
    return sky_table(key)[0]


def draw_offset(key, part):
    return sky_table(key)[1]


def draw_science(key, part):
    coadd_tiles = sky_tiles(key)
    ordering, shifts = sky_table(key)
    padded = jnp.pad(coadd_tiles, ((0, 0), (KER_HALF, KER_HALF)))
    spreads = jax.random.uniform(jax.random.fold_in(key, 14), (N_VISIT,), jnp.float32, 1.2, 2.6)
    gains = jnp.exp(jax.random.uniform(jax.random.fold_in(key, 15), (N_VISIT, N_GRP), jnp.float32, jnp.log(0.6), jnp.log(1.6)))
    levels = jax.random.uniform(jax.random.fold_in(key, 16), (N_VISIT, N_GRP), jnp.float32, -0.5, 0.5)
    noise = 0.1 * jax.random.truncated_normal(jax.random.fold_in(key, 17), -5.0, 5.0, (N_VISIT, ROWS, N_GRP * COLS), jnp.float32)
    points = jnp.arange(-KER_HALF, KER_HALF + 1).astype(jnp.float32)

    def exposure(inputs):
        tile_id, shift_rows, spread = inputs
        rows_index = (tile_id * ROWS + shift_rows - KER_HALF + jnp.arange(ROWS + 2 * KER_HALF).astype(jnp.int32)) % (N_VISIT * ROWS)
        window = jnp.take(padded, rows_index.astype(jnp.int32), axis=0)
        kernel_taps = jnp.exp(-points * points / (2.0 * spread * spread))
        kernel_taps = kernel_taps / jnp.sum(kernel_taps)
        blurred = lax.conv_general_dilated(window[None, None], kernel_taps[None, None, None, :], (1, 1), 'VALID')
        blurred = lax.conv_general_dilated(blurred, kernel_taps[None, None, :, None], (1, 1), 'VALID')
        return blurred[0, 0]
    blurred = lax.map(exposure, (ordering, shifts, spreads))
    stripe = jnp.arange(N_GRP * COLS) // COLS
    gain_cols = jnp.take(gains, stripe, axis=1)
    level_cols = jnp.take(levels, stripe, axis=1)
    result = blurred * gain_cols[:, None, :] + level_cols[:, None, :] + noise
    return result.reshape(N_VISIT * ROWS, N_GRP * COLS)


def setup_inputs(seed: int = 0) -> dict:
    keys = jax.random.split(jax.random.key(seed), 5)
    coadd_tiles = draw_coadd_tiles(jax.random.fold_in(keys[4], 71), 0)
    science = draw_science(jax.random.fold_in(keys[4], 71), 0)
    correlation = draw_correlation(jax.random.fold_in(keys[4], 71), 0)
    offset = draw_offset(jax.random.fold_in(keys[4], 71), 0)
    return dict(coadd_tiles=coadd_tiles, science=science, correlation=correlation, offset=offset)


ridge = 0.05
epsilon = 1e-06

def gauss_taps(spread, half_width):
    points = jnp.arange(-half_width, half_width + 1).astype(jnp.float32)
    return jnp.exp(-points * points / (2.0 * spread * spread))

def basis_taps():
    points = jnp.arange(-KER_HALF, KER_HALF + 1).astype(jnp.float32)
    narrow = gauss_taps(1.0, KER_HALF)
    middle = gauss_taps(1.8, KER_HALF)
    wide_gauss = gauss_taps(3.2, KER_HALF)
    slope_taps = points * middle / 1.8
    row_taps = jnp.stack([narrow, middle, wide_gauss, slope_taps, middle])
    col_taps = jnp.stack([narrow, middle, wide_gauss, middle, slope_taps])
    scales = jnp.sqrt(lax.optimization_barrier(jnp.sum(row_taps * row_taps, 1)) * lax.optimization_barrier(jnp.sum(col_taps * col_taps, 1)))
    return (row_taps / scales[:, None], col_taps)

def filter_taps():
    smooth = gauss_taps(2.0, FILT_HALF)
    return smooth / jnp.sqrt(jnp.sum(smooth * smooth))

def along_cols_ref(image_in, kernel_taps):
    result = lax.conv_general_dilated(image_in[None, None], kernel_taps[:, None, None, :], (1, 1), 'VALID', precision=lax.Precision.HIGHEST)
    return result[0]

def along_rows_ref(layers, kernel_taps):
    result = lax.conv_general_dilated(layers[None], kernel_taps[:, None, :, None], (1, 1), 'VALID', feature_group_count=layers.shape[0], precision=lax.Precision.HIGHEST)
    return result[0]

def build_normal(gram_matrix, basis_sums, counted):
    upper_rows = jnp.concatenate([gram_matrix, basis_sums[:, None]], 1)
    lower_row = jnp.concatenate([basis_sums, jnp.array([counted], jnp.float32)])[None]
    return jnp.concatenate([upper_rows, lower_row], 0) / counted + ridge * jnp.eye(BASIS + 1, dtype=jnp.float32)

def reference(coadd_tiles, science, correlation, offset):
    row_taps, col_taps = basis_taps()
    smooth = filter_taps()[None]
    strip_rows = N_VISIT * ROWS
    padded = jnp.pad(coadd_tiles, ((0, 0), (KER_HALF, KER_HALF)))
    counted = float(ROWS * COLS * N_GRP)

    def exposure(inputs):
        tile_id, shift_rows, science_rows = inputs
        first_row = tile_id * ROWS + shift_rows - KER_HALF
        rows_index = (first_row + jnp.arange(ROWS + 2 * KER_HALF).astype(jnp.int32)) % strip_rows
        window = jnp.take(padded, rows_index.astype(jnp.int32), axis=0)
        matched = along_rows_ref(along_cols_ref(window, col_taps), row_taps)
        basis_flat = matched.reshape(BASIS, -1)
        gram_matrix = jnp.dot(basis_flat, basis_flat.T, precision=lax.Precision.HIGHEST)
        basis_sums = lax.optimization_barrier(jnp.sum(basis_flat, 1))
        projection = jnp.dot(basis_flat, science_rows.reshape(-1), precision=lax.Precision.HIGHEST)
        science_total = jnp.sum(science_rows)
        normal = build_normal(gram_matrix, basis_sums, counted)
        rhs_vector = jnp.concatenate([projection, science_total[None]]) / counted
        coefficients = jnp.linalg.solve(normal, rhs_vector)
        difference = science_rows - lax.optimization_barrier(jnp.sum(coefficients[:BASIS, None, None] * matched, 0)) - coefficients[BASIS]
        wide_diff = jnp.pad(difference, ((FILT_HALF, FILT_HALF), (FILT_HALF, FILT_HALF)))
        filtered = along_rows_ref(along_cols_ref(wide_diff, smooth), smooth)[0]
        noise_power = lax.optimization_barrier(jnp.mean((difference * difference).reshape(ROWS, N_GRP, COLS), axis=(0, 2)))
        significance = filtered.reshape(ROWS, N_GRP, COLS) / jnp.sqrt(noise_power + epsilon)[None, :, None]
        return (difference, significance.reshape(ROWS, N_GRP * COLS), coefficients)
    differences, significances, coefficients = lax.map(exposure, (correlation, offset, science.reshape(N_VISIT, ROWS, N_GRP * COLS)))
    return (differences.reshape(strip_rows, N_GRP * COLS), significances.reshape(strip_rows, N_GRP * COLS), coefficients)
```

```python
import functools

import jax
import jax.numpy as jnp
import ml_dtypes
import numpy as np
from jax import lax
from jax.experimental import pallas as pl
from jax.experimental.pallas import tpu as pltpu
from jax.sharding import Mesh
from jax.sharding import PartitionSpec as P

ROWS = 256
COLS = 2048
KER_HALF = 10
BASIS = 5
FILT_HALF = 6
GRP = ("grp_0", "grp_1")
LANES = 128
HALF = 64
BLOCKS = COLS // LANES
TILES = BLOCKS + 1
WIN = 280
WIN_PAD = 288
SENT = ROWS + 8
STRIP = BLOCKS * ROWS
BAND = 160
FBAND = 144
NSUMS = 32

ridge = 0.05
epsilon = 1e-06
bf16 = jnp.bfloat16
f32 = jnp.float32
VMEM = pl.BlockSpec(memory_space=pltpu.VMEM)
SMEM = pl.BlockSpec(memory_space=pltpu.SMEM)


def params(mib):
    return pltpu.CompilerParams(vmem_limit_bytes=mib * 1024 * 1024)


def gauss_taps(spread, half_width):
    points = np.arange(-half_width, half_width + 1).astype(np.float64)
    return np.exp(-points * points / (2.0 * spread * spread))


def basis_taps():
    points = np.arange(-KER_HALF, KER_HALF + 1).astype(np.float64)
    narrow, middle, wide = (gauss_taps(s, KER_HALF) for s in (1.0, 1.8, 3.2))
    slope = points * middle / 1.8
    row = np.stack([narrow, middle, wide, slope, middle])
    col = np.stack([narrow, middle, wide, middle, slope])
    scales = np.sqrt((row * row).sum(1) * (col * col).sum(1))
    return row / scales[:, None], np.stack([narrow, middle, wide, slope])


def banded(taps, distance):
    half = (len(taps) - 1) // 2
    inside = np.abs(distance) <= half
    return np.where(inside, taps[np.clip(distance + half, 0, 2 * half)], 0.0)


def halves(matrix):
    matrix = matrix.astype(np.float32)
    high = matrix.astype(ml_dtypes.bfloat16)
    low = (matrix - high.astype(np.float32)).astype(ml_dtypes.bfloat16)
    return high, low


def constants():
    row, col = basis_taps()
    k, n = np.arange(2 * LANES)[:, None], np.arange(LANES)[None, :]
    shift = k - HALF - n
    high, low = halves(np.concatenate([banded(c, shift) for c in col], 1))
    col_mat = np.concatenate([high, high, low], 0)
    i, k = np.arange(LANES)[:, None], np.arange(BAND)[None, :]
    high, low = halves(np.concatenate([banded(row[b], k - i - KER_HALF) for b in (0, 1, 3, 2, 4)], 0))
    row_mat = np.concatenate([high, low, high], 1)
    smooth = gauss_taps(2.0, FILT_HALF)
    smooth = smooth / np.sqrt((smooth * smooth).sum())
    high, low = halves(banded(smooth, shift))
    fcol_mat = np.concatenate([high, high, low], 0)
    k = np.arange(FBAND)[None, :]
    high, low = halves(np.concatenate([banded(smooth, k - i), banded(smooth, k - 16 - i)], 0))
    frow_mat = np.concatenate([high, low, high], 1)
    return col_mat, row_mat, fcol_mat, frow_mat


COL_MAT, ROW_MAT, FCOL_MAT, FROW_MAT = constants()


def split(x):
    high = x.astype(bf16)
    return high, (x - high.astype(f32)).astype(bf16)


def pack_kernel(tile_id, shift, coadd, out):
    lane = lax.broadcasted_iota(jnp.int32, (8, LANES), 1)
    meta = jnp.where(lane == 0, tile_id[0].astype(f32), shift[0].astype(f32))
    for h in range(BLOCKS):
        out[h, :ROWS] = coadd[:, h * LANES : (h + 1) * LANES]
        out[h, ROWS:] = meta


def pick_kernel(meta, held, out, strip):
    for u in range(BLOCKS):
        strip[u * ROWS : (u + 1) * ROWS] = held[u, :ROWS]
    strip[STRIP : STRIP + ROWS] = held[0, :ROWS]
    strip[STRIP + ROWS :] = held[1, :8]

    def one(v, carry):
        first = meta[v, 0] * ROWS + meta[v, 1] - KER_HALF
        out[v] = strip[pl.ds(first, WIN), :]
        return carry

    lax.fori_loop(0, BLOCKS, one, 0)


def frame_kernel(science, left, right, out):
    def block(t):
        if t < 0:
            return left[...]
        if t == BLOCKS:
            return right[...]
        return science[:, t * LANES : (t + 1) * LANES]

    for t in range(TILES):
        out[t] = jnp.concatenate([block(t - 1)[:, HALF:], block(t)[:, :HALF]], 1)


def match_kernel(win, left, right, sci, col_mat, row_mat, matched, sums, xh, xl, acc):
    pad = jnp.zeros((WIN_PAD - WIN, LANES), f32)
    for t in range(TILES + 1):
        x = left[...] if t == 0 else right[...] if t == TILES else win[t - 1]
        xh[t], xl[t] = split(jnp.concatenate([x, pad], 0))
    acc[...] = jnp.zeros_like(acc)
    lane = lax.broadcasted_iota(jnp.int32, (8, LANES), 1)

    def layers(t):
        a_hi = jnp.concatenate([xh[t], xh[t + 1]], 1)
        a_lo = jnp.concatenate([xl[t], xl[t + 1]], 1)
        y = jnp.dot(jnp.concatenate([a_hi, a_lo, a_hi], 1), col_mat[...], preferred_element_type=f32)
        return split(y)

    def rows_of(ts):
        ys = [layers(t) for t in ts]
        for f, bases in enumerate(((0,), (1, 3), (2,), (4,))):
            lo = (0, 1, 3, 4)[f] * LANES
            lhs = row_mat[lo : lo + len(bases) * LANES, :]
            y_hi = jnp.concatenate([y[0][:, f * LANES : (f + 1) * LANES] for y in ys], 1)
            y_lo = jnp.concatenate([y[1][:, f * LANES : (f + 1) * LANES] for y in ys], 1)
            for r in range(2):
                part = slice(r * LANES, r * LANES + BAND)
                rhs = jnp.concatenate([y_hi[part], y_hi[part], y_lo[part]], 0)
                m = jnp.dot(lhs, rhs, preferred_element_type=f32)
                for i, b in enumerate(bases):
                    for s, t in enumerate(ts):
                        matched[b, t, r * LANES : (r + 1) * LANES] = m[i * LANES : (i + 1) * LANES, s * LANES : (s + 1) * LANES]

    def gram(t, keep):
        parts = [acc[k] for k in range(26)]
        for i in range(ROWS // 8):
            rows = slice(i * 8, i * 8 + 8)
            m = [matched[b, t, rows] for b in range(BASIS)]
            d = sci[t, rows]
            if keep is not None:
                m = [jnp.where(keep, x, 0.0) for x in m]
                d = jnp.where(keep, d, 0.0)
            k = 0
            for b in range(BASIS):
                for c in range(b, BASIS):
                    parts[k] = parts[k] + m[b] * m[c]
                    k += 1
            for b in range(BASIS):
                parts[15 + b] = parts[15 + b] + m[b]
                parts[20 + b] = parts[20 + b] + m[b] * d
            parts[25] = parts[25] + d
        for k in range(26):
            acc[k] = parts[k]

    def pair(p, carry):
        rows_of((2 * p, 2 * p + 1))

        @pl.when(p > 0)
        def _():
            gram(2 * p, None)

        @pl.when(p == 0)
        def _():
            gram(0, lane >= HALF)

        gram(2 * p + 1, None)
        return carry

    lax.fori_loop(0, TILES // 2, pair, 0)
    rows_of((TILES - 1,))
    gram(TILES - 1, lane < HALF)
    rows = [jnp.sum(acc[k], axis=0, keepdims=True) for k in range(26)]
    rows = jnp.concatenate(rows + [jnp.zeros((NSUMS - 26, LANES), f32)], 0)
    sums[...] = jnp.broadcast_to(jnp.sum(rows, axis=1, keepdims=True), (NSUMS, LANES))


def solve(total, counted):
    def entry(k):
        return total[k : k + 1] / counted

    m, k = {}, 0
    for b in range(BASIS):
        for c in range(b, BASIS):
            m[b, c] = entry(k)
            k += 1
    for b in range(BASIS):
        m[b, BASIS] = entry(15 + b)
    m[BASIS, BASIS] = jnp.ones((1, LANES), f32)
    n = BASIS + 1
    for b in range(n):
        m[b, b] = m[b, b] + ridge
    rhs = [entry(20 + b) for b in range(BASIS)] + [entry(25)]
    inv = []
    for a in range(n):
        inv.append(1.0 / m[a, a])
        for b in range(a + 1, n):
            factor = m[a, b] * inv[a]
            for c in range(b, n):
                m[b, c] = m[b, c] - factor * m[a, c]
            rhs[b] = rhs[b] - factor * rhs[a]
    out = [None] * n
    for a in reversed(range(n)):
        value = rhs[a]
        for b in range(a + 1, n):
            value = value - m[a, b] * out[b]
        out[a] = value * inv[a]
    return out


def finish_kernel(counted, groups, mine, other, matched, sci, fcol_mat, frow_mat, diff, sig, coef, dh, dl, eh, el, keep):
    c = solve(mine[...] + other[...], counted)
    lane = lax.broadcasted_iota(jnp.int32, (1, LANES), 1)
    coef_row = c[0]
    for b in range(1, BASIS + 1):
        coef_row = jnp.where(lane == b, c[b], coef_row)
    coef[...] = coef_row[:, : BASIS + 1]
    g = lax.axis_index(GRP[0]) * lax.axis_size(GRP[1]) + lax.axis_index(GRP[1])
    low_ok = jnp.where(g > 0, 1.0, 0.0).astype(f32)
    high_ok = jnp.where(g < groups - 1, 1.0, 0.0).astype(f32)
    low_mask = jnp.where(lane >= HALF, 1.0, low_ok)
    high_mask = jnp.where(lane < HALF, 1.0, high_ok)

    def one(t, power):
        d = sci[t] - c[BASIS]
        total = c[0] * matched[0, t]
        for b in range(1, BASIS):
            total = total + c[b] * matched[b, t]
        d = d - total
        d = d * jnp.where(t == 0, low_mask, jnp.where(t == TILES - 1, high_mask, 1.0))
        keep[t] = d
        dh[t], dl[t] = split(d)
        own = jnp.where((t == 0) & (lane < HALF), 0.0, jnp.where((t == TILES - 1) & (lane >= HALF), 0.0, 1.0))
        return power + jnp.sum((d * d * own).reshape(ROWS // 8, 8, LANES), axis=0)

    power = lax.fori_loop(0, TILES, one, jnp.zeros((8, LANES), f32))
    noise = jnp.sum(jnp.sum(power, axis=0, keepdims=True), axis=1, keepdims=True) / float(ROWS * COLS)
    scale = 1.0 / jnp.sqrt(jnp.broadcast_to(noise, (1, LANES)) + epsilon)

    def along_rows(ts):
        d_hi = jnp.concatenate([dh[t] for t in ts], 1)
        d_lo = jnp.concatenate([dl[t] for t in ts], 1)
        for r in range(2):
            part = slice(0, FBAND) if r == 0 else slice(ROWS - FBAND, ROWS)
            rhs = jnp.concatenate([d_hi[part], d_hi[part], d_lo[part]], 0)
            e = jnp.dot(frow_mat[r * LANES : (r + 1) * LANES, :], rhs, preferred_element_type=f32)
            e_hi, e_lo = split(e)
            for s, t in enumerate(ts):
                eh[t, r * LANES : (r + 1) * LANES] = e_hi[:, s * LANES : (s + 1) * LANES]
                el[t, r * LANES : (r + 1) * LANES] = e_lo[:, s * LANES : (s + 1) * LANES]

    def rows_pair(p, carry):
        along_rows((2 * p, 2 * p + 1))
        return carry

    lax.fori_loop(0, TILES // 2, rows_pair, 0)
    along_rows((TILES - 1,))
    for j in range(BLOCKS):
        e_hi = jnp.concatenate([eh[j], eh[j + 1]], 1)
        e_lo = jnp.concatenate([el[j], el[j + 1]], 1)
        s = jnp.dot(jnp.concatenate([e_hi, e_lo, e_hi], 1), fcol_mat[...], preferred_element_type=f32)
        sig[:, j * LANES : (j + 1) * LANES] = s * scale
        diff[:, j * LANES : (j + 1) * LANES] = jnp.concatenate([keep[j][:, HALF:], keep[j + 1][:, :HALF]], 1)


def call(kernel, ins, outs, scratch=(), mib=48, flops=0, nbytes=0):
    return pl.pallas_call(
        kernel,
        out_shape=outs,
        in_specs=ins,
        out_specs=jax.tree.map(lambda _: VMEM, outs),
        scratch_shapes=list(scratch),
        compiler_params=params(mib),
        cost_estimate=pl.CostEstimate(flops=flops, bytes_accessed=nbytes, transcendentals=0),
    )


def shape(*dims, dtype=f32):
    return jax.ShapeDtypeStruct(dims, dtype)


def line(size):
    up = [(i, i + 1) for i in range(size - 1)]
    return up, [(j, i) for i, j in up]


def shards(coadd, science, correlation, offset):
    groups = lax.axis_size(GRP)
    up, down = line(groups)
    sent = call(pack_kernel, [SMEM, SMEM, VMEM], shape(BLOCKS, SENT, LANES), nbytes=4 << 20)(correlation, offset, coadd)
    held = lax.all_to_all(sent, "visit", 0, 0, tiled=True)
    sci_left = lax.ppermute(science[:, COLS - LANES :], GRP, up)
    sci_right = lax.ppermute(science[:, :LANES], GRP, down)
    framed = call(frame_kernel, [VMEM] * 3, shape(TILES, ROWS, LANES), nbytes=4 << 20)(science, sci_left, sci_right)
    meta = held[:, ROWS, :2].astype(jnp.int32)
    picked = call(
        pick_kernel, [SMEM, VMEM], shape(BLOCKS, WIN, LANES), [pltpu.VMEM((STRIP + ROWS + 8, LANES), f32)], nbytes=5 << 20
    )(meta, held)
    win = lax.all_to_all(picked, "visit", 0, 0, tiled=True)
    left = lax.ppermute(win[BLOCKS - 1], GRP, up)
    right = lax.ppermute(win[0], GRP, down)
    tile16 = pltpu.VMEM((TILES + 1, WIN_PAD, LANES), bf16)
    matched, sums = call(
        match_kernel,
        [VMEM] * 6,
        (shape(BASIS, TILES, ROWS, LANES), shape(NSUMS, LANES)),
        [tile16, tile16, pltpu.VMEM((26, 8, LANES), f32)],
        flops=8 << 30,
    )(win, left, right, framed, jnp.asarray(COL_MAT), jnp.asarray(ROW_MAT))
    for axis, swap in ((GRP[1], [(0, 1), (1, 0)]), (GRP[0], [(0, 1), (1, 0), (2, 3), (3, 2)])):
        sums = sums + lax.ppermute(sums, axis, swap)
    other = lax.ppermute(sums, GRP[0], [(0, 3), (3, 0), (1, 2), (2, 1)])
    block16 = pltpu.VMEM((TILES, ROWS, LANES), bf16)
    return call(
        functools.partial(finish_kernel, float(ROWS * COLS * groups), groups),
        [VMEM] * 6,
        (shape(ROWS, COLS), shape(ROWS, COLS), shape(1, BASIS + 1)),
        [block16] * 4 + [pltpu.VMEM((TILES, ROWS, LANES), f32)],
        flops=3 << 30,
    )(sums, other, matched, framed, jnp.asarray(FCOL_MAT), jnp.asarray(FROW_MAT))


def solution(mesh):
    split_mesh = Mesh(mesh.devices.reshape(mesh.shape["visit"], 4, 2), ("visit", "grp_0", "grp_1"))
    in_specs = (P("visit", GRP), P("visit", GRP), P("visit"), P("visit"))
    out_specs = (P("visit", GRP), P("visit", GRP), P("visit", None))
    return jax.shard_map(shards, mesh=split_mesh, in_specs=in_specs, out_specs=out_specs, check_vma=False)
```

```python
import functools

import jax
import jax.numpy as jnp
import ml_dtypes
import numpy as np
from jax import lax
from jax.experimental import pallas as pl
from jax.experimental.pallas import tpu as pltpu
from jax.sharding import Mesh
from jax.sharding import PartitionSpec as P

ROWS = 256
COLS = 2048
KER_HALF = 10
BASIS = 5
FILT_HALF = 6
GRP = ("grp_0", "grp_1")
LANES = 128
HALF = 64
BLOCKS = COLS // LANES
TILES = BLOCKS + 1
WIN = 280
WIN_PAD = 288
SENT = ROWS + 8
STRIP = BLOCKS * ROWS
BAND = 160
FBAND = 144
NSUMS = 32
EDGE = 16
PAIRS = (TILES - 3) // 2
PARTS = 4

ridge = 0.05
epsilon = 1e-06
bf16 = jnp.bfloat16
f32 = jnp.float32
VMEM = pl.BlockSpec(memory_space=pltpu.VMEM)
SMEM = pl.BlockSpec(memory_space=pltpu.SMEM)


def params(mib):
    return pltpu.CompilerParams(vmem_limit_bytes=mib * 1024 * 1024)


def gauss_taps(spread, half_width):
    points = np.arange(-half_width, half_width + 1).astype(np.float64)
    return np.exp(-points * points / (2.0 * spread * spread))


def basis_taps():
    points = np.arange(-KER_HALF, KER_HALF + 1).astype(np.float64)
    narrow, middle, wide = (gauss_taps(s, KER_HALF) for s in (1.0, 1.8, 3.2))
    slope = points * middle / 1.8
    row = np.stack([narrow, middle, wide, slope, middle])
    col = np.stack([narrow, middle, wide, middle, slope])
    scales = np.sqrt((row * row).sum(1) * (col * col).sum(1))
    return row / scales[:, None], np.stack([narrow, middle, wide, slope])


def banded(taps, distance):
    half = (len(taps) - 1) // 2
    inside = np.abs(distance) <= half
    return np.where(inside, taps[np.clip(distance + half, 0, 2 * half)], 0.0)


def halves(matrix):
    matrix = matrix.astype(np.float32)
    high = matrix.astype(ml_dtypes.bfloat16)
    low = (matrix - high.astype(np.float32)).astype(ml_dtypes.bfloat16)
    return high, low


def constants():
    row, col = basis_taps()
    k, n = np.arange(2 * LANES)[:, None], np.arange(LANES)[None, :]
    shift = k - HALF - n
    high, low = halves(np.concatenate([banded(c, shift) for c in col], 1))
    col_mat = np.concatenate([high, high, low], 0)
    i, k = np.arange(LANES)[:, None], np.arange(BAND)[None, :]
    high, low = halves(np.concatenate([banded(row[b], k - i - KER_HALF) for b in (0, 1, 3, 2, 4)], 0))
    row_mat = np.concatenate([high, low, high], 1)
    smooth = gauss_taps(2.0, FILT_HALF)
    smooth = smooth / np.sqrt((smooth * smooth).sum())
    high, low = halves(banded(smooth, shift))
    fcol_mat = np.concatenate([high, high, low], 0)
    k = np.arange(FBAND)[None, :]
    high, low = halves(np.concatenate([banded(smooth, k - i), banded(smooth, k - 16 - i)], 0))
    frow_mat = np.concatenate([high, low, high], 1)
    return col_mat, row_mat, fcol_mat, frow_mat


COL_MAT, ROW_MAT, FCOL_MAT, FROW_MAT = constants()


def split(x):
    high = x.astype(bf16)
    return high, (x - high.astype(f32)).astype(bf16)


def edge_kernel(coadd_first, coadd_last, sci_first, sci_last, to_left, to_right):
    to_left[:EDGE] = jnp.transpose(coadd_first[...])[:EDGE]
    to_left[EDGE:] = jnp.transpose(sci_first[...])[:EDGE]
    to_right[:EDGE] = jnp.transpose(coadd_last[...])[LANES - EDGE :]
    to_right[EDGE:] = jnp.transpose(sci_last[...])[LANES - EDGE :]


def pack_kernel(tile_id, shift, coadd, from_left, from_right, out):
    lane = lax.broadcasted_iota(jnp.int32, (4, LANES), 1)
    meta = jnp.where(lane == 0, tile_id[0].astype(f32), shift[0].astype(f32))
    for h in range(BLOCKS):
        out[h, :ROWS] = coadd[:, h * LANES : (h + 1) * LANES]
        source = from_left if h < BLOCKS // 2 else from_right
        k = 2 * h % EDGE
        pieces = [source[k + i : k + i + 1, q * LANES : (q + 1) * LANES] for i in range(2) for q in range(2)]
        out[h, ROWS:] = jnp.concatenate(pieces + [meta], 0)


def pick_kernel(meta, held, out, strip, edges):
    def keep_edges(u, at):
        for i in range(2):
            for q in range(2):
                row = ROWS + 2 * i + q
                edges[i : i + 1, at * ROWS + q * LANES : at * ROWS + (q + 1) * LANES] = held[u, row : row + 1]

    edges[...] = jnp.zeros_like(edges)
    for u in range(BLOCKS):
        strip[u * ROWS : (u + 1) * ROWS] = held[u, :ROWS]
        keep_edges(u, u)
    strip[STRIP : STRIP + ROWS] = held[0, :ROWS]
    strip[STRIP + ROWS :] = held[1, :8]
    keep_edges(0, BLOCKS)
    keep_edges(1, BLOCKS + 1)

    def one(v, carry):
        base = pl.multiple_of(meta[v, 0] * ROWS, ROWS)
        skip = meta[v, 1] - KER_HALF
        out[v, :WIN] = strip[pl.ds(base + skip, WIN), :]
        wide = edges[:, pl.ds(base, 5 * LANES)]
        wide = pltpu.roll(wide, 5 * LANES - skip, 1)
        pieces = [wide[i : i + 1, q * LANES : (q + 1) * LANES] for i in range(2) for q in range(3)]
        out[v, WIN:] = jnp.concatenate(pieces + [wide[2:4, :LANES]], 0)
        return carry

    lax.fori_loop(0, BLOCKS, one, 0)


def frame_kernel(science, from_left, from_right, out, side):
    side[...] = jnp.zeros_like(side)
    side[:EDGE] = from_right[EDGE:]
    side[LANES - EDGE :] = from_left[EDGE:]
    edge = jnp.transpose(side[...])

    def block(t):
        return edge if t in (-1, BLOCKS) else science[:, t * LANES : (t + 1) * LANES]

    for t in range(TILES):
        out[t] = jnp.concatenate([block(t - 1)[:, HALF:], block(t)[:, :HALF]], 1)


def match_kernel(win, sci, col_mat, row_mat, matched, sums, xh, xl, acc, side):
    pad = jnp.zeros((WIN_PAD - WIN, LANES), f32)
    side[...] = jnp.zeros_like(side)
    for h in range(BLOCKS):
        for i in range(2):
            row = 2 * h + i
            row = row + LANES - EDGE if row < EDGE else row - EDGE
            for q in range(3):
                side[row : row + 1, q * LANES : (q + 1) * LANES] = win[h, WIN + 3 * i + q : WIN + 3 * i + q + 1]
    edge = jnp.transpose(side[...])[:WIN]
    for t in range(TILES + 1):
        x = edge if t in (0, TILES) else win[t - 1, :WIN]
        xh[t], xl[t] = split(jnp.concatenate([x, pad], 0))
    acc[...] = jnp.zeros_like(acc)
    lane = lax.broadcasted_iota(jnp.int32, (8, LANES), 1)

    def layers(t):
        a_hi = jnp.concatenate([xh[t], xh[t + 1]], 1)
        a_lo = jnp.concatenate([xl[t], xl[t + 1]], 1)
        y = jnp.dot(jnp.concatenate([a_hi, a_lo, a_hi], 1), col_mat[...], preferred_element_type=f32)
        return split(y)

    def rows_of(ts):
        ys = [layers(t) for t in ts]
        for f, bases in enumerate(((0,), (1, 3), (2,), (4,))):
            lo = (0, 1, 3, 4)[f] * LANES
            lhs = row_mat[lo : lo + len(bases) * LANES, :]
            y_hi = jnp.concatenate([y[0][:, f * LANES : (f + 1) * LANES] for y in ys], 1)
            y_lo = jnp.concatenate([y[1][:, f * LANES : (f + 1) * LANES] for y in ys], 1)
            for r in range(2):
                part = slice(r * LANES, r * LANES + BAND)
                rhs = jnp.concatenate([y_hi[part], y_hi[part], y_lo[part]], 0)
                m = jnp.dot(lhs, rhs, preferred_element_type=f32)
                for i, b in enumerate(bases):
                    for s, t in enumerate(ts):
                        matched[b, t, r * LANES : (r + 1) * LANES] = m[i * LANES : (i + 1) * LANES, s * LANES : (s + 1) * LANES]

    def gram(tiles):
        parts = [acc[k] for k in range(26)]
        for tile in tiles:
            for i in range(ROWS // 8):
                rows = slice(i * 8, i * 8 + 8)
                if isinstance(tile, tuple):
                    m = [jnp.where(lane >= HALF, matched[b, tile[0], rows], matched[b, tile[1], rows]) for b in range(BASIS)]
                    d = jnp.where(lane >= HALF, sci[tile[0], rows], sci[tile[1], rows])
                else:
                    m = [matched[b, tile, rows] for b in range(BASIS)]
                    d = sci[tile, rows]
                k = 0
                for b in range(BASIS):
                    for c in range(b, BASIS):
                        parts[k] = parts[k] + m[b] * m[c]
                        k += 1
                for b in range(BASIS):
                    parts[15 + b] = parts[15 + b] + m[b]
                    parts[20 + b] = parts[20 + b] + m[b] * d
                parts[25] = parts[25] + d
        for k in range(26):
            acc[k] = parts[k]

    rows_of((1, 2))

    def pair(p, carry):
        gram((2 * p - 1, 2 * p))
        rows_of((2 * p + 1, 2 * p + 2))
        return carry

    lax.fori_loop(1, PAIRS, pair, 0)
    gram((TILES - 4, TILES - 3))
    rows_of((0, TILES - 1))
    gram(((0, TILES - 1),))
    rows_of((TILES - 2,))
    gram((TILES - 2,))
    rows = [jnp.sum(acc[k], axis=0, keepdims=True) for k in range(26)]
    rows = jnp.concatenate(rows + [jnp.zeros((NSUMS - 26, LANES), f32)], 0)
    total = jnp.broadcast_to(jnp.sum(rows, axis=1, keepdims=True), (NSUMS, LANES))
    packed = total[:8]
    for q in range(1, 4):
        packed = jnp.where(lane >= 32 * q, total[8 * q : 8 * q + 8], packed)
    for g in range(sums.shape[0]):
        sums[g] = packed


def solve(total, counted):
    def entry(k):
        return total[k : k + 1] / counted

    m, k = {}, 0
    for b in range(BASIS):
        for c in range(b, BASIS):
            m[b, c] = entry(k)
            k += 1
    for b in range(BASIS):
        m[b, BASIS] = entry(15 + b)
    m[BASIS, BASIS] = jnp.ones((1, LANES), f32)
    n = BASIS + 1
    for b in range(n):
        m[b, b] = m[b, b] + ridge
    rhs = [entry(20 + b) for b in range(BASIS)] + [entry(25)]
    inv = []
    for a in range(n):
        inv.append(1.0 / m[a, a])
        for b in range(a + 1, n):
            factor = m[a, b] * inv[a]
            for c in range(b, n):
                m[b, c] = m[b, c] - factor * m[a, c]
            rhs[b] = rhs[b] - factor * rhs[a]
    out = [None] * n
    for a in reversed(range(n)):
        value = rhs[a]
        for b in range(a + 1, n):
            value = value - m[a, b] * out[b]
        out[a] = value * inv[a]
    return out


def finish_kernel(counted, groups, sums, matched, sci, fcol_mat, frow_mat, diff, sig, coef, eh, el, keep, dout, sout, sems):
    packed = jnp.sum(sums[...], axis=0)
    spread = [jnp.broadcast_to(packed[:, 32 * q : 32 * q + 1], (8, LANES)) for q in range(4)]
    c = solve(jnp.concatenate(spread, 0), counted)
    lane = lax.broadcasted_iota(jnp.int32, (1, LANES), 1)
    coef_row = c[0]
    for b in range(1, BASIS + 1):
        coef_row = jnp.where(lane == b, c[b], coef_row)
    coef[...] = coef_row[:, : BASIS + 1]
    g = lax.axis_index(GRP[0]) * lax.axis_size(GRP[1]) + lax.axis_index(GRP[1])
    low_ok = jnp.where(g > 0, 1.0, 0.0).astype(f32)
    high_ok = jnp.where(g < groups - 1, 1.0, 0.0).astype(f32)

    def squares(d):
        return jnp.sum((d * d).reshape(ROWS // 8, 8, LANES), axis=0)

    def residual(t):
        total = c[0] * matched[0, t]
        for b in range(1, BASIS):
            total = total + c[b] * matched[b, t]
        d = sci[t] - total - c[BASIS]
        keep[t] = d
        return d

    def along_rows(ts, ds):
        halves = [split(d) for d in ds]
        d_hi = jnp.concatenate([x[0] for x in halves], 1)
        d_lo = jnp.concatenate([x[1] for x in halves], 1)
        for r in range(2):
            part = slice(0, FBAND) if r == 0 else slice(ROWS - FBAND, ROWS)
            rhs = jnp.concatenate([d_hi[part], d_hi[part], d_lo[part]], 0)
            e = jnp.dot(frow_mat[r * LANES : (r + 1) * LANES, :], rhs, preferred_element_type=f32)
            e_hi, e_lo = split(e)
            for s, t in enumerate(ts):
                eh[t, r * LANES : (r + 1) * LANES] = e_hi[:, s * LANES : (s + 1) * LANES]
                el[t, r * LANES : (r + 1) * LANES] = e_lo[:, s * LANES : (s + 1) * LANES]

    def pair(p, power):
        ts = (2 * p + 1, 2 * p + 2)
        ds = [residual(t) for t in ts]
        along_rows(ts, ds)
        return power + squares(ds[0]) + squares(ds[1])

    power = lax.fori_loop(0, PAIRS, pair, jnp.zeros((8, LANES), f32))
    last = residual(TILES - 2)
    along_rows((TILES - 2,), [last])
    low, high = residual(0), residual(TILES - 1)
    power = power + squares(last) + squares(jnp.where(lane >= HALF, low, high))
    low = low * jnp.where(lane >= HALF, 1.0, low_ok)
    high = high * jnp.where(lane < HALF, 1.0, high_ok)
    along_rows((0, TILES - 1), [low, high])
    noise = jnp.sum(jnp.sum(power, axis=0, keepdims=True), axis=1, keepdims=True) / float(ROWS * COLS)
    scale = 1.0 / jnp.sqrt(jnp.broadcast_to(noise, (1, LANES)) + epsilon)

    copies = []
    for q in range(PARTS):
        part = slice(q * COLS // PARTS, (q + 1) * COLS // PARTS)
        for j in range(q * BLOCKS // PARTS, (q + 1) * BLOCKS // PARTS):
            e_hi = jnp.concatenate([eh[j], eh[j + 1]], 1)
            e_lo = jnp.concatenate([el[j], el[j + 1]], 1)
            s = jnp.dot(jnp.concatenate([e_hi, e_lo, e_hi], 1), fcol_mat[...], preferred_element_type=f32)
            sout[:, j * LANES : (j + 1) * LANES] = s * scale
            dout[:, j * LANES : (j + 1) * LANES] = jnp.concatenate([keep[j][:, HALF:], keep[j + 1][:, :HALF]], 1)
        copies.append(pltpu.make_async_copy(sout.at[:, part], sig.at[:, part], sems.at[2 * q]))
        copies.append(pltpu.make_async_copy(dout.at[:, part], diff.at[:, part], sems.at[2 * q + 1]))
        copies[-1].start()
        copies[-2].start()
    for copy in copies:
        copy.wait()


def call(kernel, ins, outs, scratch=(), mib=8, flops=0, nbytes=0, out_specs=None, **more):
    return pl.pallas_call(
        kernel,
        out_shape=outs,
        in_specs=ins,
        out_specs=jax.tree.map(lambda _: VMEM, outs) if out_specs is None else out_specs,
        scratch_shapes=list(scratch),
        compiler_params=params(mib),
        cost_estimate=pl.CostEstimate(flops=flops, bytes_accessed=nbytes, transcendentals=0),
        **more,
    )


def shape(*dims, dtype=f32):
    return jax.ShapeDtypeStruct(dims, dtype)


def line(size):
    up = [(i, i + 1) for i in range(size - 1)]
    return up, [(j, i) for i, j in up]


def shards(coadd, science, correlation, offset):
    groups = lax.axis_size(GRP)
    up, down = line(groups)
    first = pl.BlockSpec((ROWS, LANES), lambda i: (0, 0))
    last = pl.BlockSpec((ROWS, LANES), lambda i: (0, BLOCKS - 1))
    whole = pl.BlockSpec((2 * EDGE, ROWS), lambda i: (0, 0))
    to_left, to_right = call(
        edge_kernel, [first, last, first, last], (shape(2 * EDGE, ROWS),) * 2, out_specs=[whole, whole], grid=(1,)
    )(coadd, coadd, science, science)
    from_left = lax.ppermute(to_right, GRP, up)
    from_right = lax.ppermute(to_left, GRP, down)
    sent = call(pack_kernel, [SMEM, SMEM, VMEM, VMEM, VMEM], shape(BLOCKS, SENT, LANES), nbytes=4 << 20)(
        correlation, offset, coadd, from_left, from_right
    )
    held = lax.all_to_all(sent, "visit", 0, 0, tiled=True)
    framed = call(
        frame_kernel, [VMEM] * 3, shape(TILES, ROWS, LANES), [pltpu.VMEM((LANES, ROWS), f32)], nbytes=4 << 20
    )(science, from_left, from_right)
    meta = held[:, ROWS + 4, :2].astype(jnp.int32)
    picked = call(
        pick_kernel,
        [SMEM, VMEM],
        shape(BLOCKS, WIN + 8, LANES),
        [pltpu.VMEM((STRIP + ROWS + 8, LANES), f32), pltpu.VMEM((8, STRIP + 2 * ROWS), f32)],
        nbytes=5 << 20,
    )(meta, held)
    win = lax.all_to_all(picked, "visit", 0, 0, tiled=True)
    tile16 = pltpu.VMEM((TILES + 1, WIN_PAD, LANES), bf16)
    matched, sums = call(
        match_kernel,
        [VMEM] * 4,
        (shape(BASIS, TILES, ROWS, LANES), shape(groups, 8, LANES)),
        [tile16, tile16, pltpu.VMEM((26, 8, LANES), f32), pltpu.VMEM((LANES, 3 * LANES), f32)],
        flops=8 << 30,
        mib=12,
    )(win, framed, jnp.asarray(COL_MAT), jnp.asarray(ROW_MAT))
    sums = lax.all_to_all(sums, GRP, 0, 0, tiled=True)
    block16 = pltpu.VMEM((TILES, ROWS, LANES), bf16)
    image = pltpu.VMEM((ROWS, COLS), f32)
    anywhere = pl.BlockSpec(memory_space=pl.ANY)
    return call(
        functools.partial(finish_kernel, float(ROWS * COLS * groups), groups),
        [VMEM] * 5,
        (shape(ROWS, COLS), shape(ROWS, COLS), shape(1, BASIS + 1)),
        [block16] * 2
        + [pltpu.VMEM((TILES, ROWS, LANES), f32), image, image, pltpu.SemaphoreType.DMA((2 * PARTS,))],
        flops=3 << 30,
        mib=16,
        out_specs=(anywhere, anywhere, VMEM),
    )(sums, matched, framed, jnp.asarray(FCOL_MAT), jnp.asarray(FROW_MAT))


def solution(mesh):
    split_mesh = Mesh(mesh.devices.reshape(mesh.shape["visit"], 4, 2), ("visit", "grp_0", "grp_1"))
    in_specs = (P("visit", GRP), P("visit", GRP), P("visit"), P("visit"))
    out_specs = (P("visit", GRP), P("visit", GRP), P("visit", None))
    return jax.shard_map(shards, mesh=split_mesh, in_specs=in_specs, out_specs=out_specs, check_vma=False)
```

```python
import functools

import jax
import jax.numpy as jnp
import ml_dtypes
import numpy as np
from jax import lax
from jax.experimental import pallas as pl
from jax.experimental.pallas import tpu as pltpu
from jax.sharding import Mesh
from jax.sharding import PartitionSpec as P

ROWS = 256
COLS = 2048
KER_HALF = 10
BASIS = 5
FILT_HALF = 6
GRP = ("grp_0", "grp_1")
LANES = 128
HALF = 64
BLOCKS = COLS // LANES
TILES = BLOCKS + 1
WIN = 280
WIN_PAD = 288
SENT = ROWS + 8
STRIP = BLOCKS * ROWS
BAND = 160
FBAND = 144
NSUMS = 32
EDGE = 16
PAIRS = (TILES - 3) // 2
PARTS = 4

ridge = 0.05
epsilon = 1e-06
bf16 = jnp.bfloat16
f32 = jnp.float32
VMEM = pl.BlockSpec(memory_space=pltpu.VMEM)
SMEM = pl.BlockSpec(memory_space=pltpu.SMEM)


def params(mib):
    return pltpu.CompilerParams(vmem_limit_bytes=mib * 1024 * 1024)


def gauss_taps(spread, half_width):
    points = np.arange(-half_width, half_width + 1).astype(np.float64)
    return np.exp(-points * points / (2.0 * spread * spread))


def basis_taps():
    points = np.arange(-KER_HALF, KER_HALF + 1).astype(np.float64)
    narrow, middle, wide = (gauss_taps(s, KER_HALF) for s in (1.0, 1.8, 3.2))
    slope = points * middle / 1.8
    row = np.stack([narrow, middle, wide, slope, middle])
    col = np.stack([narrow, middle, wide, middle, slope])
    scales = np.sqrt((row * row).sum(1) * (col * col).sum(1))
    return row / scales[:, None], np.stack([narrow, middle, wide, slope])


def banded(taps, distance):
    half = (len(taps) - 1) // 2
    inside = np.abs(distance) <= half
    return np.where(inside, taps[np.clip(distance + half, 0, 2 * half)], 0.0)


def halves(matrix):
    matrix = matrix.astype(np.float32)
    high = matrix.astype(ml_dtypes.bfloat16)
    low = (matrix - high.astype(np.float32)).astype(ml_dtypes.bfloat16)
    return high, low


def constants():
    row, col = basis_taps()
    k, n = np.arange(2 * LANES)[:, None], np.arange(LANES)[None, :]
    shift = k - HALF - n
    high, low = halves(np.concatenate([banded(c, shift) for c in col], 1))
    col_mat = np.concatenate([high, high, low], 0)
    i, k = np.arange(LANES)[:, None], np.arange(BAND)[None, :]
    high, low = halves(np.concatenate([banded(row[b], k - i - KER_HALF) for b in (0, 1, 3, 2, 4)], 0))
    row_mat = np.concatenate([high, low, high], 1)
    smooth = gauss_taps(2.0, FILT_HALF)
    smooth = smooth / np.sqrt((smooth * smooth).sum())
    high, low = halves(banded(smooth, shift))
    fcol_mat = np.concatenate([high, high, low], 0)
    k = np.arange(FBAND)[None, :]
    high, low = halves(np.concatenate([banded(smooth, k - i), banded(smooth, k - 16 - i)], 0))
    frow_mat = np.concatenate([high, low, high], 1)
    return col_mat, row_mat, fcol_mat, frow_mat


COL_MAT, ROW_MAT, FCOL_MAT, FROW_MAT = constants()


def split(x):
    high = x.astype(bf16)
    return high, (x - high.astype(f32)).astype(bf16)


def edge_kernel(coadd_first, coadd_last, sci_first, sci_last, to_left, to_right):
    to_left[:EDGE] = jnp.transpose(coadd_first[...])[:EDGE]
    to_left[EDGE:] = jnp.transpose(sci_first[...])[:EDGE]
    to_right[:EDGE] = jnp.transpose(coadd_last[...])[LANES - EDGE :]
    to_right[EDGE:] = jnp.transpose(sci_last[...])[LANES - EDGE :]


def pack_kernel(tile_id, shift, coadd, out):
    lane = lax.broadcasted_iota(jnp.int32, (8, LANES), 1)
    meta = jnp.where(lane == 0, tile_id[0].astype(f32), shift[0].astype(f32))
    for h in range(BLOCKS):
        out[h, :ROWS] = coadd[:, h * LANES : (h + 1) * LANES]
        out[h, ROWS:] = meta


def patch_kernel(packed, from_left, from_right, out):
    for h in range(BLOCKS):
        source = from_left if h < BLOCKS // 2 else from_right
        k = 2 * h % EDGE
        for i in range(2):
            for q in range(2):
                row = ROWS + 2 * i + q
                out[h, row : row + 1] = source[k + i : k + i + 1, q * LANES : (q + 1) * LANES]


def pick_kernel(meta, held, out, strip, edges):
    def keep_edges(u, at):
        for i in range(2):
            for q in range(2):
                row = ROWS + 2 * i + q
                edges[i : i + 1, at * ROWS + q * LANES : at * ROWS + (q + 1) * LANES] = held[u, row : row + 1]

    edges[...] = jnp.zeros_like(edges)
    for u in range(BLOCKS):
        strip[u * ROWS : (u + 1) * ROWS] = held[u, :ROWS]
        keep_edges(u, u)
    strip[STRIP : STRIP + ROWS] = held[0, :ROWS]
    strip[STRIP + ROWS :] = held[1, :8]
    keep_edges(0, BLOCKS)
    keep_edges(1, BLOCKS + 1)

    def one(v, carry):
        base = pl.multiple_of(meta[v, 0] * ROWS, ROWS)
        skip = meta[v, 1] - KER_HALF
        out[v, :WIN] = strip[pl.ds(base + skip, WIN), :]
        wide = edges[:, pl.ds(base, 5 * LANES)]
        wide = pltpu.roll(wide, 5 * LANES - skip, 1)
        pieces = [wide[i : i + 1, q * LANES : (q + 1) * LANES] for i in range(2) for q in range(3)]
        out[v, WIN:] = jnp.concatenate(pieces + [wide[2:4, :LANES]], 0)
        return carry

    lax.fori_loop(0, BLOCKS, one, 0)


def match_kernel(win, science, from_left, from_right, col_mat, row_mat, matched, sci, sums, xh, xl, acc, side):
    pad = jnp.zeros((WIN_PAD - WIN, LANES), f32)
    side[...] = jnp.zeros_like(side)
    for h in range(BLOCKS):
        for i in range(2):
            row = 2 * h + i
            row = row + LANES - EDGE if row < EDGE else row - EDGE
            for q in range(3):
                side[row : row + 1, q * LANES : (q + 1) * LANES] = win[h, WIN + 3 * i + q : WIN + 3 * i + q + 1]
    edge = jnp.transpose(side[...])[:WIN]
    for t in range(TILES + 1):
        x = edge if t in (0, TILES) else win[t - 1, :WIN]
        xh[t], xl[t] = split(jnp.concatenate([x, pad], 0))
    side[:, :ROWS] = jnp.zeros((LANES, ROWS), f32)
    side[:EDGE, :ROWS] = from_right[EDGE:]
    side[LANES - EDGE :, :ROWS] = from_left[EDGE:]
    sci_edge = jnp.transpose(side[:, :ROWS])
    sci[0] = jnp.concatenate([sci_edge[:, HALF:], science[:, :HALF]], 1)
    sci[TILES - 1] = jnp.concatenate([science[:, COLS - HALF :], sci_edge[:, :HALF]], 1)
    acc[...] = jnp.zeros_like(acc)
    lane = lax.broadcasted_iota(jnp.int32, (8, LANES), 1)

    def layers(t):
        a_hi = jnp.concatenate([xh[t], xh[t + 1]], 1)
        a_lo = jnp.concatenate([xl[t], xl[t + 1]], 1)
        y = jnp.dot(jnp.concatenate([a_hi, a_lo, a_hi], 1), col_mat[...], preferred_element_type=f32)
        return split(y)

    def frame(t):
        at = (t - 1) * LANES
        if not isinstance(t, int):
            at = pl.multiple_of(at, LANES)
        wide = science[:, pl.ds(at, 2 * LANES)]
        sci[t] = jnp.concatenate([wide[:, HALF:LANES], wide[:, LANES : LANES + HALF]], 1)

    def rows_of(ts):
        for t in ts:
            if not isinstance(t, int) or 0 < t < TILES - 1:
                frame(t)
        ys = [layers(t) for t in ts]
        for f, bases in enumerate(((0,), (1, 3), (2,), (4,))):
            lo = (0, 1, 3, 4)[f] * LANES
            lhs = row_mat[lo : lo + len(bases) * LANES, :]
            y_hi = jnp.concatenate([y[0][:, f * LANES : (f + 1) * LANES] for y in ys], 1)
            y_lo = jnp.concatenate([y[1][:, f * LANES : (f + 1) * LANES] for y in ys], 1)
            for r in range(2):
                part = slice(r * LANES, r * LANES + BAND)
                rhs = jnp.concatenate([y_hi[part], y_hi[part], y_lo[part]], 0)
                m = jnp.dot(lhs, rhs, preferred_element_type=f32)
                for i, b in enumerate(bases):
                    for s, t in enumerate(ts):
                        matched[b, t, r * LANES : (r + 1) * LANES] = m[i * LANES : (i + 1) * LANES, s * LANES : (s + 1) * LANES]

    def gram(tiles):
        parts = [acc[k] for k in range(26)]
        for tile in tiles:
            for i in range(ROWS // 8):
                rows = slice(i * 8, i * 8 + 8)
                if isinstance(tile, tuple):
                    m = [jnp.where(lane >= HALF, matched[b, tile[0], rows], matched[b, tile[1], rows]) for b in range(BASIS)]
                    d = jnp.where(lane >= HALF, sci[tile[0], rows], sci[tile[1], rows])
                else:
                    m = [matched[b, tile, rows] for b in range(BASIS)]
                    d = sci[tile, rows]
                k = 0
                for b in range(BASIS):
                    for c in range(b, BASIS):
                        parts[k] = parts[k] + m[b] * m[c]
                        k += 1
                for b in range(BASIS):
                    parts[15 + b] = parts[15 + b] + m[b]
                    parts[20 + b] = parts[20 + b] + m[b] * d
                parts[25] = parts[25] + d
        for k in range(26):
            acc[k] = parts[k]

    rows_of((1, 2))

    def pair(p, carry):
        gram((2 * p - 1, 2 * p))
        rows_of((2 * p + 1, 2 * p + 2))
        return carry

    lax.fori_loop(1, PAIRS, pair, 0)
    gram((TILES - 4, TILES - 3))
    rows_of((0, TILES - 1))
    gram(((0, TILES - 1),))
    rows_of((TILES - 2,))
    gram((TILES - 2,))
    rows = [jnp.sum(acc[k], axis=0, keepdims=True) for k in range(26)]
    rows = jnp.concatenate(rows + [jnp.zeros((NSUMS - 26, LANES), f32)], 0)
    total = jnp.broadcast_to(jnp.sum(rows, axis=1, keepdims=True), (NSUMS, LANES))
    packed = total[:8]
    for q in range(1, 4):
        packed = jnp.where(lane >= 32 * q, total[8 * q : 8 * q + 8], packed)
    for g in range(sums.shape[0]):
        sums[g] = packed


def solve(total, counted):
    def entry(k):
        return total[k : k + 1] / counted

    m, k = {}, 0
    for b in range(BASIS):
        for c in range(b, BASIS):
            m[b, c] = entry(k)
            k += 1
    for b in range(BASIS):
        m[b, BASIS] = entry(15 + b)
    m[BASIS, BASIS] = jnp.ones((1, LANES), f32)
    n = BASIS + 1
    for b in range(n):
        m[b, b] = m[b, b] + ridge
    rhs = [entry(20 + b) for b in range(BASIS)] + [entry(25)]
    inv = []
    for a in range(n):
        inv.append(1.0 / m[a, a])
        for b in range(a + 1, n):
            factor = m[a, b] * inv[a]
            for c in range(b, n):
                m[b, c] = m[b, c] - factor * m[a, c]
            rhs[b] = rhs[b] - factor * rhs[a]
    out = [None] * n
    for a in reversed(range(n)):
        value = rhs[a]
        for b in range(a + 1, n):
            value = value - m[a, b] * out[b]
        out[a] = value * inv[a]
    return out


def finish_kernel(counted, groups, sums, matched, sci, fcol_mat, frow_mat, diff, sig, coef, eh, el, keep, dout, sout, sems):
    packed = jnp.sum(sums[...], axis=0)
    spread = [jnp.broadcast_to(packed[:, 32 * q : 32 * q + 1], (8, LANES)) for q in range(4)]
    c = solve(jnp.concatenate(spread, 0), counted)
    lane = lax.broadcasted_iota(jnp.int32, (1, LANES), 1)
    coef_row = c[0]
    for b in range(1, BASIS + 1):
        coef_row = jnp.where(lane == b, c[b], coef_row)
    coef[...] = coef_row[:, : BASIS + 1]
    g = lax.axis_index(GRP[0]) * lax.axis_size(GRP[1]) + lax.axis_index(GRP[1])
    low_ok = jnp.where(g > 0, 1.0, 0.0).astype(f32)
    high_ok = jnp.where(g < groups - 1, 1.0, 0.0).astype(f32)

    def squares(d):
        return jnp.sum((d * d).reshape(ROWS // 8, 8, LANES), axis=0)

    def residual(t):
        total = c[0] * matched[0, t]
        for b in range(1, BASIS):
            total = total + c[b] * matched[b, t]
        d = sci[t] - total - c[BASIS]
        keep[t] = d
        return d

    def along_rows(ts, ds):
        halves = [split(d) for d in ds]
        d_hi = jnp.concatenate([x[0] for x in halves], 1)
        d_lo = jnp.concatenate([x[1] for x in halves], 1)
        for r in range(2):
            part = slice(0, FBAND) if r == 0 else slice(ROWS - FBAND, ROWS)
            rhs = jnp.concatenate([d_hi[part], d_hi[part], d_lo[part]], 0)
            e = jnp.dot(frow_mat[r * LANES : (r + 1) * LANES, :], rhs, preferred_element_type=f32)
            e_hi, e_lo = split(e)
            for s, t in enumerate(ts):
                eh[t, r * LANES : (r + 1) * LANES] = e_hi[:, s * LANES : (s + 1) * LANES]
                el[t, r * LANES : (r + 1) * LANES] = e_lo[:, s * LANES : (s + 1) * LANES]

    def pair(p, power):
        ts = (2 * p + 1, 2 * p + 2)
        ds = [residual(t) for t in ts]
        along_rows(ts, ds)
        return power + squares(ds[0]) + squares(ds[1])

    power = lax.fori_loop(0, PAIRS, pair, jnp.zeros((8, LANES), f32))
    last = residual(TILES - 2)
    along_rows((TILES - 2,), [last])
    low, high = residual(0), residual(TILES - 1)
    power = power + squares(last) + squares(jnp.where(lane >= HALF, low, high))
    low = low * jnp.where(lane >= HALF, 1.0, low_ok)
    high = high * jnp.where(lane < HALF, 1.0, high_ok)
    along_rows((0, TILES - 1), [low, high])
    noise = jnp.sum(jnp.sum(power, axis=0, keepdims=True), axis=1, keepdims=True) / float(ROWS * COLS)
    scale = 1.0 / jnp.sqrt(jnp.broadcast_to(noise, (1, LANES)) + epsilon)

    copies = []
    for q in range(PARTS):
        part = slice(q * COLS // PARTS, (q + 1) * COLS // PARTS)
        for j in range(q * BLOCKS // PARTS, (q + 1) * BLOCKS // PARTS):
            e_hi = jnp.concatenate([eh[j], eh[j + 1]], 1)
            e_lo = jnp.concatenate([el[j], el[j + 1]], 1)
            s = jnp.dot(jnp.concatenate([e_hi, e_lo, e_hi], 1), fcol_mat[...], preferred_element_type=f32)
            sout[:, j * LANES : (j + 1) * LANES] = s * scale
            dout[:, j * LANES : (j + 1) * LANES] = jnp.concatenate([keep[j][:, HALF:], keep[j + 1][:, :HALF]], 1)
        copies.append(pltpu.make_async_copy(sout.at[:, part], sig.at[:, part], sems.at[2 * q]))
        copies.append(pltpu.make_async_copy(dout.at[:, part], diff.at[:, part], sems.at[2 * q + 1]))
        copies[-1].start()
        copies[-2].start()
    for copy in copies:
        copy.wait()


def call(kernel, ins, outs, scratch=(), mib=8, flops=0, nbytes=0, out_specs=None, **more):
    return pl.pallas_call(
        kernel,
        out_shape=outs,
        in_specs=ins,
        out_specs=jax.tree.map(lambda _: VMEM, outs) if out_specs is None else out_specs,
        scratch_shapes=list(scratch),
        compiler_params=params(mib),
        cost_estimate=pl.CostEstimate(flops=flops, bytes_accessed=nbytes, transcendentals=0),
        **more,
    )


def shape(*dims, dtype=f32):
    return jax.ShapeDtypeStruct(dims, dtype)


def line(size):
    up = [(i, i + 1) for i in range(size - 1)]
    return up, [(j, i) for i, j in up]


def shards(coadd, science, correlation, offset):
    groups = lax.axis_size(GRP)
    up, down = line(groups)
    mats = [jnp.asarray(m) for m in (COL_MAT, ROW_MAT, FCOL_MAT, FROW_MAT)]
    to_left, to_right = call(edge_kernel, [VMEM] * 4, (shape(2 * EDGE, ROWS),) * 2)(
        coadd[:, :LANES], coadd[:, COLS - LANES :], science[:, :LANES], science[:, COLS - LANES :]
    )
    from_left = lax.ppermute(to_right, GRP, up)
    from_right = lax.ppermute(to_left, GRP, down)
    coadd, _, _ = lax.optimization_barrier((coadd, to_left, to_right))
    packed = call(pack_kernel, [SMEM, SMEM, VMEM], shape(BLOCKS, SENT, LANES), flops=1 << 20, nbytes=4 << 20)(
        correlation, offset, coadd
    )
    sent = call(patch_kernel, [VMEM] * 3, shape(BLOCKS, SENT, LANES), input_output_aliases={0: 0})(
        packed, from_left, from_right
    )
    held = lax.all_to_all(sent, "visit", 0, 0, tiled=True)
    meta = held[:, ROWS + 4, :2].astype(jnp.int32)
    picked = call(
        pick_kernel,
        [SMEM, VMEM],
        shape(BLOCKS, WIN + 8, LANES),
        [pltpu.VMEM((STRIP + ROWS + 8, LANES), f32), pltpu.VMEM((8, STRIP + 2 * ROWS), f32)],
        nbytes=5 << 20,
    )(meta, held)
    win = lax.all_to_all(picked, "visit", 0, 0, tiled=True)
    tile16 = pltpu.VMEM((TILES + 1, WIN_PAD, LANES), bf16)
    matched, framed, sums = call(
        match_kernel,
        [VMEM] * 6,
        (shape(BASIS, TILES, ROWS, LANES), shape(TILES, ROWS, LANES), shape(groups, 8, LANES)),
        [tile16, tile16, pltpu.VMEM((26, 8, LANES), f32), pltpu.VMEM((LANES, 3 * LANES), f32)],
        flops=8 << 30,
        mib=12,
    )(win, science, from_left, from_right, *mats[:2])
    sums = lax.all_to_all(sums, GRP, 0, 0, tiled=True)
    block16 = pltpu.VMEM((TILES, ROWS, LANES), bf16)
    image = pltpu.VMEM((ROWS, COLS), f32)
    anywhere = pl.BlockSpec(memory_space=pl.ANY)
    return call(
        functools.partial(finish_kernel, float(ROWS * COLS * groups), groups),
        [VMEM] * 5,
        (shape(ROWS, COLS), shape(ROWS, COLS), shape(1, BASIS + 1)),
        [block16] * 2
        + [pltpu.VMEM((TILES, ROWS, LANES), f32), image, image, pltpu.SemaphoreType.DMA((2 * PARTS,))],
        flops=3 << 30,
        mib=16,
        out_specs=(anywhere, anywhere, VMEM),
    )(sums, matched, framed, *mats[2:])


def solution(mesh):
    split_mesh = Mesh(mesh.devices.reshape(mesh.shape["visit"], 4, 2), ("visit", "grp_0", "grp_1"))
    in_specs = (P("visit", GRP), P("visit", GRP), P("visit"), P("visit"))
    out_specs = (P("visit", GRP), P("visit", GRP), P("visit", None))
    return jax.shard_map(shards, mesh=split_mesh, in_specs=in_specs, out_specs=out_specs, check_vma=False)
```

```python
import functools

import jax
import jax.numpy as jnp
import ml_dtypes
import numpy as np
from jax import lax
from jax.experimental import pallas as pl
from jax.experimental.pallas import tpu as pltpu
from jax.sharding import Mesh
from jax.sharding import PartitionSpec as P

ROWS = 256
COLS = 2048
KER_HALF = 10
BASIS = 5
FILT_HALF = 6
GRP = ("grp_0", "grp_1")
LANES = 128
HALF = 64
BLOCKS = COLS // LANES
TILES = BLOCKS + 1
WIN = 280
WIN_PAD = 288
SENT = ROWS + 8
STRIP = BLOCKS * ROWS
BAND = 160
FBAND = 144
NSUMS = 32
EDGE = 16
PAIRS = (TILES - 3) // 2
PARTS = 4

ridge = 0.05
epsilon = 1e-06
bf16 = jnp.bfloat16
f32 = jnp.float32
VMEM = pl.BlockSpec(memory_space=pltpu.VMEM)
SMEM = pl.BlockSpec(memory_space=pltpu.SMEM)


def params(mib):
    return pltpu.CompilerParams(vmem_limit_bytes=mib * 1024 * 1024)


def gauss_taps(spread, half_width):
    points = np.arange(-half_width, half_width + 1).astype(np.float64)
    return np.exp(-points * points / (2.0 * spread * spread))


def basis_taps():
    points = np.arange(-KER_HALF, KER_HALF + 1).astype(np.float64)
    narrow, middle, wide = (gauss_taps(s, KER_HALF) for s in (1.0, 1.8, 3.2))
    slope = points * middle / 1.8
    row = np.stack([narrow, middle, wide, slope, middle])
    col = np.stack([narrow, middle, wide, middle, slope])
    scales = np.sqrt((row * row).sum(1) * (col * col).sum(1))
    return row / scales[:, None], np.stack([narrow, middle, wide, slope])


def banded(taps, distance):
    half = (len(taps) - 1) // 2
    inside = np.abs(distance) <= half
    return np.where(inside, taps[np.clip(distance + half, 0, 2 * half)], 0.0)


def halves(matrix):
    matrix = matrix.astype(np.float32)
    high = matrix.astype(ml_dtypes.bfloat16)
    low = (matrix - high.astype(np.float32)).astype(ml_dtypes.bfloat16)
    return high, low


def constants():
    row, col = basis_taps()
    k, n = np.arange(2 * LANES)[:, None], np.arange(LANES)[None, :]
    shift = k - HALF - n
    high, low = halves(np.concatenate([banded(c, shift) for c in col], 1))
    col_mat = np.concatenate([high, high, low], 0)
    i, k = np.arange(LANES)[:, None], np.arange(BAND)[None, :]
    high, low = halves(np.concatenate([banded(row[b], k - i - KER_HALF) for b in (0, 1, 3, 2, 4)], 0))
    row_mat = np.concatenate([high, low, high], 1)
    smooth = gauss_taps(2.0, FILT_HALF)
    smooth = smooth / np.sqrt((smooth * smooth).sum())
    high, low = halves(banded(smooth, shift))
    fcol_mat = np.concatenate([high, high, low], 0)
    k = np.arange(FBAND)[None, :]
    high, low = halves(np.concatenate([banded(smooth, k - i), banded(smooth, k - 16 - i)], 0))
    frow_mat = np.concatenate([high, low, high], 1)
    return col_mat, row_mat, fcol_mat, frow_mat


COL_MAT, ROW_MAT, FCOL_MAT, FROW_MAT = constants()


def split(x):
    high = x.astype(bf16)
    return high, (x - high.astype(f32)).astype(bf16)


def edge_kernel(coadd, science, to_left, to_right, tiles, sems):
    first, last = slice(0, LANES), slice(COLS - LANES, COLS)
    copies = []
    for k, (source, part) in enumerate(((coadd, first), (science, first), (coadd, last), (science, last))):
        copies.append(pltpu.make_async_copy(source.at[:, part], tiles.at[k], sems.at[k]))
        copies[-1].start()
    for copy in copies:
        copy.wait()
    to_left[:EDGE] = jnp.transpose(tiles[0])[:EDGE]
    to_left[EDGE:] = jnp.transpose(tiles[1])[:EDGE]
    to_right[:EDGE] = jnp.transpose(tiles[2])[LANES - EDGE :]
    to_right[EDGE:] = jnp.transpose(tiles[3])[LANES - EDGE :]


def pack_kernel(tile_id, shift, coadd, out):
    lane = lax.broadcasted_iota(jnp.int32, (8, LANES), 1)
    meta = jnp.where(lane == 0, tile_id[0].astype(f32), shift[0].astype(f32))
    for h in range(BLOCKS):
        out[h, :ROWS] = coadd[:, h * LANES : (h + 1) * LANES]
        out[h, ROWS:] = meta


def patch_kernel(packed, from_left, from_right, out):
    for h in range(BLOCKS):
        source = from_left if h < BLOCKS // 2 else from_right
        k = 2 * h % EDGE
        for i in range(2):
            for q in range(2):
                row = ROWS + 2 * i + q
                out[h, row : row + 1] = source[k + i : k + i + 1, q * LANES : (q + 1) * LANES]


def pick_kernel(meta, held, out, strip, edges):
    def keep_edges(u, at):
        for i in range(2):
            for q in range(2):
                row = ROWS + 2 * i + q
                edges[i : i + 1, at * ROWS + q * LANES : at * ROWS + (q + 1) * LANES] = held[u, row : row + 1]

    edges[...] = jnp.zeros_like(edges)
    for u in range(BLOCKS):
        strip[u * ROWS : (u + 1) * ROWS] = held[u, :ROWS]
        keep_edges(u, u)
    strip[STRIP : STRIP + ROWS] = held[0, :ROWS]
    strip[STRIP + ROWS :] = held[1, :8]
    keep_edges(0, BLOCKS)
    keep_edges(1, BLOCKS + 1)

    for v in range(BLOCKS):
        base = pl.multiple_of(meta[v, 0] * ROWS, ROWS)
        skip = meta[v, 1] - KER_HALF
        out[v, :WIN] = strip[pl.ds(base + skip, WIN), :]
        wide = edges[:, pl.ds(base, 5 * LANES)]
        wide = pltpu.roll(wide, 5 * LANES - skip, 1)
        pieces = [wide[i : i + 1, q * LANES : (q + 1) * LANES] for i in range(2) for q in range(3)]
        out[v, WIN:] = jnp.concatenate(pieces + [wide[2:4, :LANES]], 0)


def match_kernel(win, science, from_left, from_right, col_mat, row_mat, matched, sci, sums, xh, xl, acc, side):
    pad = jnp.zeros((WIN_PAD - WIN, LANES), f32)
    side[...] = jnp.zeros_like(side)
    for h in range(BLOCKS):
        for i in range(2):
            row = 2 * h + i
            row = row + LANES - EDGE if row < EDGE else row - EDGE
            for q in range(3):
                side[row : row + 1, q * LANES : (q + 1) * LANES] = win[h, WIN + 3 * i + q : WIN + 3 * i + q + 1]
    edge = jnp.transpose(side[...])[:WIN]
    for t in range(TILES + 1):
        x = edge if t in (0, TILES) else win[t - 1, :WIN]
        xh[t], xl[t] = split(jnp.concatenate([x, pad], 0))
    side[:, :ROWS] = jnp.zeros((LANES, ROWS), f32)
    side[:EDGE, :ROWS] = from_right[EDGE:]
    side[LANES - EDGE :, :ROWS] = from_left[EDGE:]
    sci_edge = jnp.transpose(side[:, :ROWS])
    sci[0] = jnp.concatenate([sci_edge[:, HALF:], science[:, :HALF]], 1)
    sci[TILES - 1] = jnp.concatenate([science[:, COLS - HALF :], sci_edge[:, :HALF]], 1)
    acc[...] = jnp.zeros_like(acc)
    lane = lax.broadcasted_iota(jnp.int32, (8, LANES), 1)

    def layers(t):
        a_hi = jnp.concatenate([xh[t], xh[t + 1]], 1)
        a_lo = jnp.concatenate([xl[t], xl[t + 1]], 1)
        y = jnp.dot(jnp.concatenate([a_hi, a_lo, a_hi], 1), col_mat[...], preferred_element_type=f32)
        return split(y)

    def frame(t):
        at = (t - 1) * LANES
        if not isinstance(t, int):
            at = pl.multiple_of(at, LANES)
        wide = science[:, pl.ds(at, 2 * LANES)]
        sci[t] = jnp.concatenate([wide[:, HALF:LANES], wide[:, LANES : LANES + HALF]], 1)

    def rows_of(ts, steps=()):
        steps = list(steps)

        def advance():
            if steps:
                steps.pop(0)()

        for t in ts:
            if not isinstance(t, int) or 0 < t < TILES - 1:
                frame(t)
        ys = []
        for t in ts:
            ys.append(layers(t))
            advance()
        for f, bases in enumerate(((0,), (1, 3), (2,), (4,))):
            lo = (0, 1, 3, 4)[f] * LANES
            lhs = row_mat[lo : lo + len(bases) * LANES, :]
            y_hi = jnp.concatenate([y[0][:, f * LANES : (f + 1) * LANES] for y in ys], 1)
            y_lo = jnp.concatenate([y[1][:, f * LANES : (f + 1) * LANES] for y in ys], 1)
            for r in range(2):
                part = slice(r * LANES, r * LANES + BAND)
                rhs = jnp.concatenate([y_hi[part], y_hi[part], y_lo[part]], 0)
                m = jnp.dot(lhs, rhs, preferred_element_type=f32)
                for i, b in enumerate(bases):
                    for s, t in enumerate(ts):
                        matched[b, t, r * LANES : (r + 1) * LANES] = m[i * LANES : (i + 1) * LANES, s * LANES : (s + 1) * LANES]
                advance()
        while steps:
            advance()

    def gram(tiles, count=10):
        work = [(tile, i) for tile in tiles for i in range(ROWS // 8)]
        size = -(-len(work) // count)
        return [functools.partial(gram_of, work[k : k + size]) for k in range(0, len(work), size)]

    def gram_of(work):
        parts = [acc[k] for k in range(26)]
        for tile, i in work:
            rows = slice(i * 8, i * 8 + 8)
            if isinstance(tile, tuple):
                m = [jnp.where(lane >= HALF, matched[b, tile[0], rows], matched[b, tile[1], rows]) for b in range(BASIS)]
                d = jnp.where(lane >= HALF, sci[tile[0], rows], sci[tile[1], rows])
            else:
                m = [matched[b, tile, rows] for b in range(BASIS)]
                d = sci[tile, rows]
            k = 0
            for b in range(BASIS):
                for c in range(b, BASIS):
                    parts[k] = parts[k] + m[b] * m[c]
                    k += 1
            for b in range(BASIS):
                parts[15 + b] = parts[15 + b] + m[b]
                parts[20 + b] = parts[20 + b] + m[b] * d
            parts[25] = parts[25] + d
        for k in range(26):
            acc[k] = parts[k]

    rows_of((1, 2))

    def pair(p, carry):
        rows_of((2 * p + 1, 2 * p + 2), gram((2 * p - 1, 2 * p)))
        return carry

    lax.fori_loop(1, PAIRS, pair, 0)
    rows_of((0, TILES - 1), gram((TILES - 4, TILES - 3)))
    rows_of((TILES - 2,), gram(((0, TILES - 1),)))
    for step in gram((TILES - 2,), 1):
        step()
    rows = [jnp.sum(acc[k], axis=0, keepdims=True) for k in range(26)]
    rows = jnp.concatenate(rows + [jnp.zeros((NSUMS - 26, LANES), f32)], 0)
    total = jnp.broadcast_to(jnp.sum(rows, axis=1, keepdims=True), (NSUMS, LANES))
    packed = total[:8]
    for q in range(1, 4):
        packed = jnp.where(lane >= 32 * q, total[8 * q : 8 * q + 8], packed)
    for g in range(sums.shape[0]):
        sums[g] = packed


def solve(total, counted):
    def entry(k):
        return total[k : k + 1] / counted

    m, k = {}, 0
    for b in range(BASIS):
        for c in range(b, BASIS):
            m[b, c] = entry(k)
            k += 1
    for b in range(BASIS):
        m[b, BASIS] = entry(15 + b)
    m[BASIS, BASIS] = jnp.ones((1, LANES), f32)
    n = BASIS + 1
    for b in range(n):
        m[b, b] = m[b, b] + ridge
    rhs = [entry(20 + b) for b in range(BASIS)] + [entry(25)]
    inv = []
    for a in range(n):
        inv.append(1.0 / m[a, a])
        for b in range(a + 1, n):
            factor = m[a, b] * inv[a]
            for c in range(b, n):
                m[b, c] = m[b, c] - factor * m[a, c]
            rhs[b] = rhs[b] - factor * rhs[a]
    out = [None] * n
    for a in reversed(range(n)):
        value = rhs[a]
        for b in range(a + 1, n):
            value = value - m[a, b] * out[b]
        out[a] = value * inv[a]
    return out


def finish_kernel(counted, groups, sums, matched, sci, fcol_mat, frow_mat, diff, sig, coef, eh, el, keep, dout, sout, sems):
    packed = jnp.sum(sums[...], axis=0)
    spread = [jnp.broadcast_to(packed[:, 32 * q : 32 * q + 1], (8, LANES)) for q in range(4)]
    c = solve(jnp.concatenate(spread, 0), counted)
    lane = lax.broadcasted_iota(jnp.int32, (1, LANES), 1)
    coef_row = c[0]
    for b in range(1, BASIS + 1):
        coef_row = jnp.where(lane == b, c[b], coef_row)
    coef[...] = coef_row[:, : BASIS + 1]
    g = lax.axis_index(GRP[0]) * lax.axis_size(GRP[1]) + lax.axis_index(GRP[1])
    low_ok = jnp.where(g > 0, 1.0, 0.0).astype(f32)
    high_ok = jnp.where(g < groups - 1, 1.0, 0.0).astype(f32)

    def squares(d):
        return jnp.sum((d * d).reshape(ROWS // 8, 8, LANES), axis=0)

    def residual(t):
        total = c[0] * matched[0, t]
        for b in range(1, BASIS):
            total = total + c[b] * matched[b, t]
        d = sci[t] - total - c[BASIS]
        keep[t] = d
        return d

    def along_rows(ts, ds):
        halves = [split(d) for d in ds]
        d_hi = jnp.concatenate([x[0] for x in halves], 1)
        d_lo = jnp.concatenate([x[1] for x in halves], 1)
        for r in range(2):
            part = slice(0, FBAND) if r == 0 else slice(ROWS - FBAND, ROWS)
            rhs = jnp.concatenate([d_hi[part], d_hi[part], d_lo[part]], 0)
            e = jnp.dot(frow_mat[r * LANES : (r + 1) * LANES, :], rhs, preferred_element_type=f32)
            e_hi, e_lo = split(e)
            for s, t in enumerate(ts):
                eh[t, r * LANES : (r + 1) * LANES] = e_hi[:, s * LANES : (s + 1) * LANES]
                el[t, r * LANES : (r + 1) * LANES] = e_lo[:, s * LANES : (s + 1) * LANES]

    def emit(j):
        at = j * LANES if isinstance(j, int) else pl.multiple_of(j * LANES, LANES)
        dout[:, pl.ds(at, LANES)] = jnp.concatenate([keep[j][:, HALF:], keep[j + 1][:, :HALF]], 1)

    def send(source, target, first, end, sem):
        part = slice(first * LANES, end * LANES)
        copy = pltpu.make_async_copy(source.at[:, part], target.at[:, part], sems.at[sem])
        copy.start()
        return copy

    def pair(p, power):
        ts = (2 * p + 1, 2 * p + 2)
        ds = [residual(t) for t in ts]
        along_rows(ts, ds)
        emit(2 * p)
        emit(2 * p + 1)
        return power + squares(ds[0]) + squares(ds[1])

    low, high = residual(0), residual(TILES - 1)
    power = squares(jnp.where(lane >= HALF, low, high))
    low = low * jnp.where(lane >= HALF, 1.0, low_ok)
    high = high * jnp.where(lane < HALF, 1.0, high_ok)
    along_rows((0, TILES - 1), [low, high])
    middle = PAIRS // 2
    power = lax.fori_loop(0, middle, pair, power)
    copies = [send(dout, diff, 0, 2 * middle, 0)]
    power = lax.fori_loop(middle, PAIRS, pair, power)
    last = residual(TILES - 2)
    along_rows((TILES - 2,), [last])
    power = power + squares(last)
    emit(BLOCKS - 2)
    emit(BLOCKS - 1)
    copies.append(send(dout, diff, 2 * middle, BLOCKS, 1))
    noise = jnp.sum(jnp.sum(power, axis=0, keepdims=True), axis=1, keepdims=True) / float(ROWS * COLS)
    scale = 1.0 / jnp.sqrt(jnp.broadcast_to(noise, (1, LANES)) + epsilon)

    each = BLOCKS // PARTS
    for q in range(PARTS):
        for j in range(q * each, (q + 1) * each):
            e_hi = jnp.concatenate([eh[j], eh[j + 1]], 1)
            e_lo = jnp.concatenate([el[j], el[j + 1]], 1)
            s = jnp.dot(jnp.concatenate([e_hi, e_lo, e_hi], 1), fcol_mat[...], preferred_element_type=f32)
            sout[:, j * LANES : (j + 1) * LANES] = s * scale
        copies.append(send(sout, sig, q * each, (q + 1) * each, 2 + q))
    for copy in copies:
        copy.wait()


def call(kernel, ins, outs, scratch=(), mib=12, flops=0, nbytes=0, out_specs=None, **more):
    return pl.pallas_call(
        kernel,
        out_shape=outs,
        in_specs=ins,
        out_specs=jax.tree.map(lambda _: VMEM, outs) if out_specs is None else out_specs,
        scratch_shapes=list(scratch),
        compiler_params=params(mib),
        cost_estimate=pl.CostEstimate(flops=flops, bytes_accessed=nbytes, transcendentals=0),
        **more,
    )


def shape(*dims, dtype=f32):
    return jax.ShapeDtypeStruct(dims, dtype)


def line(size):
    up = [(i, i + 1) for i in range(size - 1)]
    return up, [(j, i) for i, j in up]


def shards(coadd, science, correlation, offset):
    groups = lax.axis_size(GRP)
    up, down = line(groups)
    mats = [jnp.asarray(m) for m in (COL_MAT, ROW_MAT, FCOL_MAT, FROW_MAT)]
    to_left, to_right = call(
        edge_kernel,
        [pl.BlockSpec(memory_space=pl.ANY)] * 2,
        (shape(2 * EDGE, ROWS),) * 2,
        [pltpu.VMEM((4, ROWS, LANES), f32), pltpu.SemaphoreType.DMA((4,))],
        mib=58,
    )(coadd, science)
    from_left = lax.ppermute(to_right, GRP, up)
    from_right = lax.ppermute(to_left, GRP, down)
    coadd, _, _ = lax.optimization_barrier((coadd, to_left, to_right))
    packed = call(pack_kernel, [SMEM, SMEM, VMEM], shape(BLOCKS, SENT, LANES), flops=1 << 20, nbytes=4 << 20)(
        correlation, offset, coadd
    )
    sent = call(patch_kernel, [VMEM] * 3, shape(BLOCKS, SENT, LANES), input_output_aliases={0: 0})(
        packed, from_left, from_right
    )
    held = lax.all_to_all(sent, "visit", 0, 0, tiled=True)
    meta = held[:, ROWS + 4, :2].astype(jnp.int32)
    picked = call(
        pick_kernel,
        [SMEM, VMEM],
        shape(BLOCKS, WIN + 8, LANES),
        [pltpu.VMEM((STRIP + ROWS + 8, LANES), f32), pltpu.VMEM((8, STRIP + 2 * ROWS), f32)],
        nbytes=5 << 20,
    )(meta, held)
    win = lax.all_to_all(picked, "visit", 0, 0, tiled=True)
    tile16 = pltpu.VMEM((TILES + 1, WIN_PAD, LANES), bf16)
    matched, framed, sums = call(
        match_kernel,
        [VMEM] * 6,
        (shape(BASIS, TILES, ROWS, LANES), shape(TILES, ROWS, LANES), shape(groups, 8, LANES)),
        [tile16, tile16, pltpu.VMEM((26, 8, LANES), f32), pltpu.VMEM((LANES, 3 * LANES), f32)],
        flops=8 << 30,
        mib=24,
    )(win, science, from_left, from_right, *mats[:2])
    sums = lax.all_to_all(sums, GRP, 0, 0, tiled=True)
    block16 = pltpu.VMEM((TILES, ROWS, LANES), bf16)
    image = pltpu.VMEM((ROWS, COLS), f32)
    anywhere = pl.BlockSpec(memory_space=pl.ANY)
    return call(
        functools.partial(finish_kernel, float(ROWS * COLS * groups), groups),
        [VMEM] * 5,
        (shape(ROWS, COLS), shape(ROWS, COLS), shape(1, BASIS + 1)),
        [block16] * 2
        + [pltpu.VMEM((TILES, ROWS, LANES), f32), image, image, pltpu.SemaphoreType.DMA((2 + PARTS,))],
        flops=3 << 30,
        mib=30,
        out_specs=(anywhere, anywhere, VMEM),
    )(sums, matched, framed, *mats[2:])


def solution(mesh):
    split_mesh = Mesh(mesh.devices.reshape(mesh.shape["visit"], 4, 2), ("visit", "grp_0", "grp_1"))
    in_specs = (P("visit", GRP), P("visit", GRP), P("visit"), P("visit"))
    out_specs = (P("visit", GRP), P("visit", GRP), P("visit", None))
    return jax.shard_map(shards, mesh=split_mesh, in_specs=in_specs, out_specs=out_specs, check_vma=False)
```

```python
import functools

import jax
import jax.numpy as jnp
import ml_dtypes
import numpy as np
from jax import lax
from jax.experimental import pallas as pl
from jax.experimental.pallas import tpu as pltpu
from jax.sharding import Mesh
from jax.sharding import PartitionSpec as P

ROWS = 256
COLS = 2048
KER_HALF = 10
BASIS = 5
FILT_HALF = 6
GRP = ("grp_0", "grp_1")
LANES = 128
HALF = 64
BLOCKS = COLS // LANES
TILES = BLOCKS + 1
WIN = 280
WIN_PAD = 288
SENT = ROWS + 8
STRIP = BLOCKS * ROWS
BAND = 160
FBAND = 144
NSUMS = 32
EDGE = 16
PAIRS = (TILES - 3) // 2
PARTS = 4

ridge = 0.05
epsilon = 1e-06
bf16 = jnp.bfloat16
f32 = jnp.float32
VMEM = pl.BlockSpec(memory_space=pltpu.VMEM)
SMEM = pl.BlockSpec(memory_space=pltpu.SMEM)


def params(mib):
    return pltpu.CompilerParams(vmem_limit_bytes=mib * 1024 * 1024)


def gauss_taps(spread, half_width):
    points = np.arange(-half_width, half_width + 1).astype(np.float64)
    return np.exp(-points * points / (2.0 * spread * spread))


def basis_taps():
    points = np.arange(-KER_HALF, KER_HALF + 1).astype(np.float64)
    narrow, middle, wide = (gauss_taps(s, KER_HALF) for s in (1.0, 1.8, 3.2))
    slope = points * middle / 1.8
    row = np.stack([narrow, middle, wide, slope, middle])
    col = np.stack([narrow, middle, wide, middle, slope])
    scales = np.sqrt((row * row).sum(1) * (col * col).sum(1))
    return row / scales[:, None], np.stack([narrow, middle, wide, slope])


def banded(taps, distance):
    half = (len(taps) - 1) // 2
    inside = np.abs(distance) <= half
    return np.where(inside, taps[np.clip(distance + half, 0, 2 * half)], 0.0)


def halves(matrix):
    matrix = matrix.astype(np.float32)
    high = matrix.astype(ml_dtypes.bfloat16)
    low = (matrix - high.astype(np.float32)).astype(ml_dtypes.bfloat16)
    return high, low


def constants():
    row, col = basis_taps()
    k, n = np.arange(2 * LANES)[:, None], np.arange(LANES)[None, :]
    shift = k - HALF - n
    high, low = halves(np.concatenate([banded(c, shift) for c in col], 1))
    col_mat = np.concatenate([high, high, low], 0)
    i, k = np.arange(LANES)[:, None], np.arange(BAND)[None, :]
    high, low = halves(np.concatenate([banded(row[b], k - i - KER_HALF) for b in (0, 1, 3, 2, 4)], 0))
    row_mat = np.concatenate([high, low, high], 1)
    smooth = gauss_taps(2.0, FILT_HALF)
    smooth = smooth / np.sqrt((smooth * smooth).sum())
    high, low = halves(banded(smooth, shift))
    fcol_mat = np.concatenate([high, high, low], 0)
    k = np.arange(FBAND)[None, :]
    high, low = halves(np.concatenate([banded(smooth, k - i), banded(smooth, k - 16 - i)], 0))
    frow_mat = np.concatenate([high, low, high], 1)
    return col_mat, row_mat, fcol_mat, frow_mat


COL_MAT, ROW_MAT, FCOL_MAT, FROW_MAT = constants()


def split(x):
    high = x.astype(bf16)
    return high, (x - high.astype(f32)).astype(bf16)


def edge_kernel(coadd_first, coadd_last, sci_first, sci_last, to_left, to_right):
    to_left[:EDGE] = jnp.transpose(coadd_first[...])[:EDGE]
    to_left[EDGE:] = jnp.transpose(sci_first[...])[:EDGE]
    to_right[:EDGE] = jnp.transpose(coadd_last[...])[LANES - EDGE :]
    to_right[EDGE:] = jnp.transpose(sci_last[...])[LANES - EDGE :]


def pack_kernel(tile_id, shift, coadd, out):
    lane = lax.broadcasted_iota(jnp.int32, (8, LANES), 1)
    meta = jnp.where(lane == 0, tile_id[0].astype(f32), shift[0].astype(f32))
    for h in range(BLOCKS):
        out[h, :ROWS] = coadd[:, h * LANES : (h + 1) * LANES]
        out[h, ROWS:] = meta


def patch_kernel(groups, packed, from_left, from_right, out):
    g = lax.axis_index(GRP[0]) * lax.axis_size(GRP[1]) + lax.axis_index(GRP[1])
    low_ok = jnp.where(g > 0, 1.0, 0.0).astype(f32)
    high_ok = jnp.where(g < groups - 1, 1.0, 0.0).astype(f32)
    for h in range(BLOCKS):
        source, ok = (from_left, low_ok) if h < BLOCKS // 2 else (from_right, high_ok)
        k = 2 * h % EDGE
        for i in range(2):
            for q in range(2):
                row = ROWS + 2 * i + q
                out[h, row : row + 1] = source[k + i : k + i + 1, q * LANES : (q + 1) * LANES] * ok


def pick_kernel(meta, held, out, strip, edges):
    def keep_edges(u, at):
        for i in range(2):
            for q in range(2):
                row = ROWS + 2 * i + q
                edges[i : i + 1, at * ROWS + q * LANES : at * ROWS + (q + 1) * LANES] = held[u, row : row + 1]

    edges[...] = jnp.zeros_like(edges)
    for u in range(BLOCKS):
        strip[u * ROWS : (u + 1) * ROWS] = held[u, :ROWS]
        keep_edges(u, u)
    strip[STRIP : STRIP + ROWS] = held[0, :ROWS]
    strip[STRIP + ROWS :] = held[1, :8]
    keep_edges(0, BLOCKS)
    keep_edges(1, BLOCKS + 1)

    for v in range(BLOCKS):
        base = pl.multiple_of(meta[v, 0] * ROWS, ROWS)
        skip = meta[v, 1] - KER_HALF
        out[v, :WIN] = strip[pl.ds(base + skip, WIN), :]
        wide = edges[:, pl.ds(base, 5 * LANES)]
        wide = pltpu.roll(wide, 5 * LANES - skip, 1)
        pieces = [wide[i : i + 1, q * LANES : (q + 1) * LANES] for i in range(2) for q in range(3)]
        out[v, WIN:] = jnp.concatenate(pieces + [wide[2:4, :LANES]], 0)


def match_kernel(win, science, from_left, from_right, col_mat, row_mat, matched, sci, sums, xh, xl, acc, side):
    pad = jnp.zeros((WIN_PAD - WIN, LANES), f32)
    side[...] = jnp.zeros_like(side)
    for h in range(BLOCKS):
        for i in range(2):
            row = 2 * h + i
            row = row + LANES - EDGE if row < EDGE else row - EDGE
            for q in range(3):
                side[row : row + 1, q * LANES : (q + 1) * LANES] = win[h, WIN + 3 * i + q : WIN + 3 * i + q + 1]
    edge = jnp.transpose(side[...])[:WIN]
    for t in range(TILES + 1):
        x = edge if t in (0, TILES) else win[t - 1, :WIN]
        xh[t], xl[t] = split(jnp.concatenate([x, pad], 0))
    side[:, :ROWS] = jnp.zeros((LANES, ROWS), f32)
    side[:EDGE, :ROWS] = from_right[EDGE:]
    side[LANES - EDGE :, :ROWS] = from_left[EDGE:]
    sci_edge = jnp.transpose(side[:, :ROWS])
    sci[0] = jnp.concatenate([sci_edge[:, HALF:], science[:, :HALF]], 1)
    sci[TILES - 1] = jnp.concatenate([science[:, COLS - HALF :], sci_edge[:, :HALF]], 1)
    acc[...] = jnp.zeros_like(acc)
    lane = lax.broadcasted_iota(jnp.int32, (8, LANES), 1)

    def layers(t):
        a_hi = jnp.concatenate([xh[t], xh[t + 1]], 1)
        a_lo = jnp.concatenate([xl[t], xl[t + 1]], 1)
        y = jnp.dot(jnp.concatenate([a_hi, a_lo, a_hi], 1), col_mat[...], preferred_element_type=f32)
        return split(y)

    def frame(t):
        at = (t - 1) * LANES
        if not isinstance(t, int):
            at = pl.multiple_of(at, LANES)
        wide = science[:, pl.ds(at, 2 * LANES)]
        sci[t] = jnp.concatenate([wide[:, HALF:LANES], wide[:, LANES : LANES + HALF]], 1)

    def rows_of(ts, steps=()):
        steps = list(steps)

        def advance():
            if steps:
                steps.pop(0)()

        for t in ts:
            if not isinstance(t, int) or 0 < t < TILES - 1:
                frame(t)
        ys = []
        for t in ts:
            ys.append(layers(t))
            advance()
        for f, bases in enumerate(((0,), (1, 3), (2,), (4,))):
            lo = (0, 1, 3, 4)[f] * LANES
            lhs = row_mat[lo : lo + len(bases) * LANES, :]
            y_hi = jnp.concatenate([y[0][:, f * LANES : (f + 1) * LANES] for y in ys], 1)
            y_lo = jnp.concatenate([y[1][:, f * LANES : (f + 1) * LANES] for y in ys], 1)
            for r in range(2):
                part = slice(r * LANES, r * LANES + BAND)
                rhs = jnp.concatenate([y_hi[part], y_hi[part], y_lo[part]], 0)
                m = jnp.dot(lhs, rhs, preferred_element_type=f32)
                for i, b in enumerate(bases):
                    for s, t in enumerate(ts):
                        matched[b, t, r * LANES : (r + 1) * LANES] = m[i * LANES : (i + 1) * LANES, s * LANES : (s + 1) * LANES]
                advance()
        while steps:
            advance()

    def gram(tiles, count=10):
        work = [(tile, i) for tile in tiles for i in range(ROWS // 8)]
        size = -(-len(work) // count)
        return [functools.partial(gram_of, work[k : k + size]) for k in range(0, len(work), size)]

    def gram_of(work):
        parts = [acc[k] for k in range(26)]
        for tile, i in work:
            rows = slice(i * 8, i * 8 + 8)
            if isinstance(tile, tuple):
                m = [jnp.where(lane >= HALF, matched[b, tile[0], rows], matched[b, tile[1], rows]) for b in range(BASIS)]
                d = jnp.where(lane >= HALF, sci[tile[0], rows], sci[tile[1], rows])
            else:
                m = [matched[b, tile, rows] for b in range(BASIS)]
                d = sci[tile, rows]
            k = 0
            for b in range(BASIS):
                for c in range(b, BASIS):
                    parts[k] = parts[k] + m[b] * m[c]
                    k += 1
            for b in range(BASIS):
                parts[15 + b] = parts[15 + b] + m[b]
                parts[20 + b] = parts[20 + b] + m[b] * d
            parts[25] = parts[25] + d
        for k in range(26):
            acc[k] = parts[k]

    rows_of((1, 2))

    def pair(p, carry):
        rows_of((2 * p + 1, 2 * p + 2), gram((2 * p - 1, 2 * p)))
        return carry

    lax.fori_loop(1, PAIRS, pair, 0)
    rows_of((0, TILES - 1), gram((TILES - 4, TILES - 3)))
    rows_of((TILES - 2,), gram(((0, TILES - 1),)))
    for step in gram((TILES - 2,), 1):
        step()
    rows = [jnp.sum(acc[k], axis=0, keepdims=True) for k in range(26)]
    rows = jnp.concatenate(rows + [jnp.zeros((NSUMS - 26, LANES), f32)], 0)
    total = jnp.broadcast_to(jnp.sum(rows, axis=1, keepdims=True), (NSUMS, LANES))
    packed = total[:8]
    for q in range(1, 4):
        packed = jnp.where(lane >= 32 * q, total[8 * q : 8 * q + 8], packed)
    for g in range(sums.shape[0]):
        sums[g] = packed


def solve(total, counted):
    def entry(k):
        return total[k : k + 1] / counted

    m, k = {}, 0
    for b in range(BASIS):
        for c in range(b, BASIS):
            m[b, c] = entry(k)
            k += 1
    for b in range(BASIS):
        m[b, BASIS] = entry(15 + b)
    m[BASIS, BASIS] = jnp.ones((1, LANES), f32)
    n = BASIS + 1
    for b in range(n):
        m[b, b] = m[b, b] + ridge
    rhs = [entry(20 + b) for b in range(BASIS)] + [entry(25)]
    inv = []
    for a in range(n):
        inv.append(1.0 / m[a, a])
        for b in range(a + 1, n):
            factor = m[a, b] * inv[a]
            for c in range(b, n):
                m[b, c] = m[b, c] - factor * m[a, c]
            rhs[b] = rhs[b] - factor * rhs[a]
    out = [None] * n
    for a in reversed(range(n)):
        value = rhs[a]
        for b in range(a + 1, n):
            value = value - m[a, b] * out[b]
        out[a] = value * inv[a]
    return out


def finish_kernel(counted, groups, sums, matched, sci, fcol_mat, frow_mat, diff, sig, coef, eh, el, keep, dout, sout, sems):
    packed = jnp.sum(sums[...], axis=0)
    spread = [jnp.broadcast_to(packed[:, 32 * q : 32 * q + 1], (8, LANES)) for q in range(4)]
    c = solve(jnp.concatenate(spread, 0), counted)
    lane = lax.broadcasted_iota(jnp.int32, (1, LANES), 1)
    coef_row = c[0]
    for b in range(1, BASIS + 1):
        coef_row = jnp.where(lane == b, c[b], coef_row)
    coef[...] = coef_row[:, : BASIS + 1]
    g = lax.axis_index(GRP[0]) * lax.axis_size(GRP[1]) + lax.axis_index(GRP[1])
    low_ok = jnp.where(g > 0, 1.0, 0.0).astype(f32)
    high_ok = jnp.where(g < groups - 1, 1.0, 0.0).astype(f32)

    def squares(d):
        return jnp.sum((d * d).reshape(ROWS // 8, 8, LANES), axis=0)

    def residual(t):
        total = c[0] * matched[0, t]
        for b in range(1, BASIS):
            total = total + c[b] * matched[b, t]
        d = sci[t] - total - c[BASIS]
        keep[t] = d
        return d

    def along_rows(ts, ds):
        halves = [split(d) for d in ds]
        d_hi = jnp.concatenate([x[0] for x in halves], 1)
        d_lo = jnp.concatenate([x[1] for x in halves], 1)
        for r in range(2):
            part = slice(0, FBAND) if r == 0 else slice(ROWS - FBAND, ROWS)
            rhs = jnp.concatenate([d_hi[part], d_hi[part], d_lo[part]], 0)
            e = jnp.dot(frow_mat[r * LANES : (r + 1) * LANES, :], rhs, preferred_element_type=f32)
            e_hi, e_lo = split(e)
            for s, t in enumerate(ts):
                eh[t, r * LANES : (r + 1) * LANES] = e_hi[:, s * LANES : (s + 1) * LANES]
                el[t, r * LANES : (r + 1) * LANES] = e_lo[:, s * LANES : (s + 1) * LANES]

    def emit(j):
        at = j * LANES if isinstance(j, int) else pl.multiple_of(j * LANES, LANES)
        dout[:, pl.ds(at, LANES)] = jnp.concatenate([keep[j][:, HALF:], keep[j + 1][:, :HALF]], 1)

    def send(source, target, first, end, sem):
        part = slice(first * LANES, end * LANES)
        copy = pltpu.make_async_copy(source.at[:, part], target.at[:, part], sems.at[sem])
        copy.start()
        return copy

    def pair(p, power):
        ts = (2 * p + 1, 2 * p + 2)
        ds = [residual(t) for t in ts]
        along_rows(ts, ds)
        emit(2 * p)
        emit(2 * p + 1)
        return power + squares(ds[0]) + squares(ds[1])

    low, high = residual(0), residual(TILES - 1)
    power = squares(jnp.where(lane >= HALF, low, high))
    low = low * jnp.where(lane >= HALF, 1.0, low_ok)
    high = high * jnp.where(lane < HALF, 1.0, high_ok)
    along_rows((0, TILES - 1), [low, high])
    middle = PAIRS // 2
    power = lax.fori_loop(0, middle, pair, power)
    copies = [send(dout, diff, 0, 2 * middle, 0)]
    power = lax.fori_loop(middle, PAIRS, pair, power)
    last = residual(TILES - 2)
    along_rows((TILES - 2,), [last])
    power = power + squares(last)
    emit(BLOCKS - 2)
    emit(BLOCKS - 1)
    copies.append(send(dout, diff, 2 * middle, BLOCKS, 1))
    noise = jnp.sum(jnp.sum(power, axis=0, keepdims=True), axis=1, keepdims=True) / float(ROWS * COLS)
    scale = 1.0 / jnp.sqrt(jnp.broadcast_to(noise, (1, LANES)) + epsilon)

    each = BLOCKS // PARTS
    for q in range(PARTS):
        for j in range(q * each, (q + 1) * each):
            e_hi = jnp.concatenate([eh[j], eh[j + 1]], 1)
            e_lo = jnp.concatenate([el[j], el[j + 1]], 1)
            s = jnp.dot(jnp.concatenate([e_hi, e_lo, e_hi], 1), fcol_mat[...], preferred_element_type=f32)
            sout[:, j * LANES : (j + 1) * LANES] = s * scale
        copies.append(send(sout, sig, q * each, (q + 1) * each, 2 + q))
    for copy in copies:
        copy.wait()


def call(kernel, ins, outs, scratch=(), mib=12, flops=0, nbytes=0, out_specs=None, **more):
    return pl.pallas_call(
        kernel,
        out_shape=outs,
        in_specs=ins,
        out_specs=jax.tree.map(lambda _: VMEM, outs) if out_specs is None else out_specs,
        scratch_shapes=list(scratch),
        compiler_params=params(mib),
        cost_estimate=pl.CostEstimate(flops=flops, bytes_accessed=nbytes, transcendentals=0),
        **more,
    )


def shape(*dims, dtype=f32):
    return jax.ShapeDtypeStruct(dims, dtype)


def ring(size):
    up = [(i, (i + 1) % size) for i in range(size)]
    return up, [(j, i) for i, j in up]


def shards(coadd, science, correlation, offset):
    groups = lax.axis_size(GRP)
    up, down = ring(groups)
    mats = [jnp.asarray(m) for m in (COL_MAT, ROW_MAT, FCOL_MAT, FROW_MAT)]
    to_left, to_right = call(edge_kernel, [VMEM] * 4, (shape(2 * EDGE, ROWS),) * 2)(
        coadd[:, :LANES], coadd[:, COLS - LANES :], science[:, :LANES], science[:, COLS - LANES :]
    )
    from_left = lax.ppermute(to_right, GRP, up)
    from_right = lax.ppermute(to_left, GRP, down)
    coadd, _, _ = lax.optimization_barrier((coadd, to_left, to_right))
    packed = call(pack_kernel, [SMEM, SMEM, VMEM], shape(BLOCKS, SENT, LANES), flops=1 << 20, nbytes=4 << 20)(
        correlation, offset, coadd
    )
    sent = call(functools.partial(patch_kernel, groups), [VMEM] * 3, shape(BLOCKS, SENT, LANES), input_output_aliases={0: 0})(
        packed, from_left, from_right
    )
    held = lax.all_to_all(sent, "visit", 0, 0, tiled=True)
    meta = held[:, ROWS + 4, :2].astype(jnp.int32)
    picked = call(
        pick_kernel,
        [SMEM, VMEM],
        shape(BLOCKS, WIN + 8, LANES),
        [pltpu.VMEM((STRIP + ROWS + 8, LANES), f32), pltpu.VMEM((8, STRIP + 2 * ROWS), f32)],
        nbytes=5 << 20,
    )(meta, held)
    win = lax.all_to_all(picked, "visit", 0, 0, tiled=True)
    tile16 = pltpu.VMEM((TILES + 1, WIN_PAD, LANES), bf16)
    matched, framed, sums = call(
        match_kernel,
        [VMEM] * 6,
        (shape(BASIS, TILES, ROWS, LANES), shape(TILES, ROWS, LANES), shape(groups, 8, LANES)),
        [tile16, tile16, pltpu.VMEM((26, 8, LANES), f32), pltpu.VMEM((LANES, 3 * LANES), f32)],
        flops=8 << 30,
        mib=24,
    )(win, science, from_left, from_right, *mats[:2])
    sums = lax.all_to_all(sums, GRP, 0, 0, tiled=True)
    block16 = pltpu.VMEM((TILES, ROWS, LANES), bf16)
    image = pltpu.VMEM((ROWS, COLS), f32)
    anywhere = pl.BlockSpec(memory_space=pl.ANY)
    return call(
        functools.partial(finish_kernel, float(ROWS * COLS * groups), groups),
        [VMEM] * 5,
        (shape(ROWS, COLS), shape(ROWS, COLS), shape(1, BASIS + 1)),
        [block16] * 2
        + [pltpu.VMEM((TILES, ROWS, LANES), f32), image, image, pltpu.SemaphoreType.DMA((2 + PARTS,))],
        flops=3 << 30,
        mib=30,
        out_specs=(anywhere, anywhere, VMEM),
    )(sums, matched, framed, *mats[2:])


def solution(mesh):
    split_mesh = Mesh(mesh.devices.reshape(mesh.shape["visit"], 4, 2), ("visit", "grp_0", "grp_1"))
    in_specs = (P("visit", GRP), P("visit", GRP), P("visit"), P("visit"))
    out_specs = (P("visit", GRP), P("visit", GRP), P("visit", None))
    return jax.shard_map(shards, mesh=split_mesh, in_specs=in_specs, out_specs=out_specs, check_vma=False)
```

```python
import functools

import jax
import jax.numpy as jnp
import ml_dtypes
import numpy as np
from jax import lax
from jax.experimental import pallas as pl
from jax.experimental.pallas import tpu as pltpu
from jax.sharding import Mesh
from jax.sharding import PartitionSpec as P

ROWS = 256
COLS = 2048
KER_HALF = 10
BASIS = 5
FILT_HALF = 6
GRP = ("grp_0", "grp_1")
LANES = 128
HALF = 64
BLOCKS = COLS // LANES
TILES = BLOCKS + 1
WIN = 280
WIN_PAD = 288
SENT = ROWS + 8
STRIP = BLOCKS * ROWS
BAND = 160
FBAND = 144
NSUMS = 32
EDGE = 16
PAIRS = (TILES - 3) // 2
PARTS = 4

ridge = 0.05
epsilon = 1e-06
bf16 = jnp.bfloat16
f32 = jnp.float32
VMEM = pl.BlockSpec(memory_space=pltpu.VMEM)
SMEM = pl.BlockSpec(memory_space=pltpu.SMEM)


def params(mib):
    return pltpu.CompilerParams(vmem_limit_bytes=mib * 1024 * 1024)


def gauss_taps(spread, half_width):
    points = np.arange(-half_width, half_width + 1).astype(np.float64)
    return np.exp(-points * points / (2.0 * spread * spread))


def basis_taps():
    points = np.arange(-KER_HALF, KER_HALF + 1).astype(np.float64)
    narrow, middle, wide = (gauss_taps(s, KER_HALF) for s in (1.0, 1.8, 3.2))
    slope = points * middle / 1.8
    row = np.stack([narrow, middle, wide, slope, middle])
    col = np.stack([narrow, middle, wide, middle, slope])
    scales = np.sqrt((row * row).sum(1) * (col * col).sum(1))
    return row / scales[:, None], np.stack([narrow, middle, wide, slope])


def banded(taps, distance):
    half = (len(taps) - 1) // 2
    inside = np.abs(distance) <= half
    return np.where(inside, taps[np.clip(distance + half, 0, 2 * half)], 0.0)


def halves(matrix):
    matrix = matrix.astype(np.float32)
    high = matrix.astype(ml_dtypes.bfloat16)
    low = (matrix - high.astype(np.float32)).astype(ml_dtypes.bfloat16)
    return high, low


def constants():
    row, col = basis_taps()
    k, n = np.arange(2 * LANES)[:, None], np.arange(LANES)[None, :]
    shift = k - HALF - n
    high, low = halves(np.concatenate([banded(c, shift) for c in col], 1))
    col_mat = np.concatenate([high, high, low], 0)
    i, k = np.arange(LANES)[:, None], np.arange(BAND)[None, :]
    high, low = halves(np.concatenate([banded(row[b], k - i - KER_HALF) for b in (0, 1, 3, 2, 4)], 0))
    row_mat = np.concatenate([high, low, high], 1)
    smooth = gauss_taps(2.0, FILT_HALF)
    smooth = smooth / np.sqrt((smooth * smooth).sum())
    high, low = halves(banded(smooth, shift))
    fcol_mat = np.concatenate([high, high, low], 0)
    k = np.arange(FBAND)[None, :]
    high, low = halves(np.concatenate([banded(smooth, k - i), banded(smooth, k - 16 - i)], 0))
    frow_mat = np.concatenate([high, low, high], 1)
    return col_mat, row_mat, fcol_mat, frow_mat


COL_MAT, ROW_MAT, FCOL_MAT, FROW_MAT = constants()


def split(x):
    high = x.astype(bf16)
    return high, (x - high.astype(f32)).astype(bf16)


def edge_kernel(coadd_first, coadd_last, sci_first, sci_last, to_left, to_right):
    to_left[:EDGE] = jnp.transpose(coadd_first[...])[:EDGE]
    to_left[EDGE:] = jnp.transpose(sci_first[...])[:EDGE]
    to_right[:EDGE] = jnp.transpose(coadd_last[...])[LANES - EDGE :]
    to_right[EDGE:] = jnp.transpose(sci_last[...])[LANES - EDGE :]


def pack_kernel(tile_id, shift, coadd, out):
    lane = lax.broadcasted_iota(jnp.int32, (8, LANES), 1)
    meta = jnp.where(lane == 0, tile_id[0].astype(f32), shift[0].astype(f32))
    for h in range(BLOCKS):
        out[h, :ROWS] = coadd[:, h * LANES : (h + 1) * LANES]
        out[h, ROWS:] = meta


def patch_kernel(groups, packed, from_left, from_right, out):
    g = lax.axis_index(GRP[0]) * lax.axis_size(GRP[1]) + lax.axis_index(GRP[1])
    low_ok = jnp.where(g > 0, 1.0, 0.0).astype(f32)
    high_ok = jnp.where(g < groups - 1, 1.0, 0.0).astype(f32)
    for h in range(BLOCKS):
        source, ok = (from_left, low_ok) if h < BLOCKS // 2 else (from_right, high_ok)
        k = 2 * h % EDGE
        for i in range(2):
            for q in range(2):
                row = ROWS + 2 * i + q
                out[h, row : row + 1] = source[k + i : k + i + 1, q * LANES : (q + 1) * LANES] * ok


def pick_kernel(meta, held, out, strip, edges):
    def keep_edges(u, at):
        for i in range(2):
            for q in range(2):
                row = ROWS + 2 * i + q
                edges[i : i + 1, at * ROWS + q * LANES : at * ROWS + (q + 1) * LANES] = held[u, row : row + 1]

    edges[...] = jnp.zeros_like(edges)
    for u in range(BLOCKS):
        strip[u * ROWS : (u + 1) * ROWS] = held[u, :ROWS]
        keep_edges(u, u)
    strip[STRIP : STRIP + ROWS] = held[0, :ROWS]
    strip[STRIP + ROWS :] = held[1, :8]
    keep_edges(0, BLOCKS)
    keep_edges(1, BLOCKS + 1)

    for v in range(BLOCKS):
        base = pl.multiple_of(meta[v, 0] * ROWS, ROWS)
        skip = meta[v, 1] - KER_HALF
        out[v, :WIN] = strip[pl.ds(base + skip, WIN), :]
        wide = edges[:, pl.ds(base, 5 * LANES)]
        wide = pltpu.roll(wide, 5 * LANES - skip, 1)
        pieces = [wide[i : i + 1, q * LANES : (q + 1) * LANES] for i in range(2) for q in range(3)]
        out[v, WIN:] = jnp.concatenate(pieces + [wide[2:4, :LANES]], 0)


def match_kernel(win, science, from_left, from_right, col_mat, row_mat, matched, sci, sums, xh, xl, acc, side):
    pad = jnp.zeros((WIN_PAD - WIN, LANES), f32)
    side[...] = jnp.zeros_like(side)
    for h in range(BLOCKS):
        for i in range(2):
            row = 2 * h + i
            row = row + LANES - EDGE if row < EDGE else row - EDGE
            for q in range(3):
                side[row : row + 1, q * LANES : (q + 1) * LANES] = win[h, WIN + 3 * i + q : WIN + 3 * i + q + 1]
    edge = jnp.transpose(side[...])[:WIN]
    for t in range(TILES + 1):
        x = edge if t in (0, TILES) else win[t - 1, :WIN]
        xh[t], xl[t] = split(jnp.concatenate([x, pad], 0))
    side[:, :ROWS] = jnp.zeros((LANES, ROWS), f32)
    side[:EDGE, :ROWS] = from_right[EDGE:]
    side[LANES - EDGE :, :ROWS] = from_left[EDGE:]
    sci_edge = jnp.transpose(side[:, :ROWS])
    sci[0] = jnp.concatenate([sci_edge[:, HALF:], science[:, :HALF]], 1)
    sci[TILES - 1] = jnp.concatenate([science[:, COLS - HALF :], sci_edge[:, :HALF]], 1)
    acc[...] = jnp.zeros_like(acc)
    lane = lax.broadcasted_iota(jnp.int32, (8, LANES), 1)

    def layers(t):
        a_hi = jnp.concatenate([xh[t], xh[t + 1]], 1)
        a_lo = jnp.concatenate([xl[t], xl[t + 1]], 1)
        y = jnp.dot(jnp.concatenate([a_hi, a_lo, a_hi], 1), col_mat[...], preferred_element_type=f32)
        return split(y)

    def frame(t):
        at = (t - 1) * LANES
        if not isinstance(t, int):
            at = pl.multiple_of(at, LANES)
        wide = science[:, pl.ds(at, 2 * LANES)]
        sci[t] = jnp.concatenate([wide[:, HALF:LANES], wide[:, LANES : LANES + HALF]], 1)

    def rows_of(ts, steps=()):
        steps = list(steps)

        def advance():
            if steps:
                steps.pop(0)()

        for t in ts:
            if not isinstance(t, int) or 0 < t < TILES - 1:
                frame(t)
        ys = []
        for t in ts:
            ys.append(layers(t))
            advance()
        for f, bases in enumerate(((0,), (1, 3), (2,), (4,))):
            lo = (0, 1, 3, 4)[f] * LANES
            lhs = row_mat[lo : lo + len(bases) * LANES, :]
            y_hi = jnp.concatenate([y[0][:, f * LANES : (f + 1) * LANES] for y in ys], 1)
            y_lo = jnp.concatenate([y[1][:, f * LANES : (f + 1) * LANES] for y in ys], 1)
            for r in range(2):
                part = slice(r * LANES, r * LANES + BAND)
                rhs = jnp.concatenate([y_hi[part], y_hi[part], y_lo[part]], 0)
                m = jnp.dot(lhs, rhs, preferred_element_type=f32)
                for i, b in enumerate(bases):
                    for s, t in enumerate(ts):
                        matched[b, t, r * LANES : (r + 1) * LANES] = m[i * LANES : (i + 1) * LANES, s * LANES : (s + 1) * LANES]
                advance()
        while steps:
            advance()

    def gram(tiles, count=10):
        work = [(tile, i) for tile in tiles for i in range(ROWS // 8)]
        size = -(-len(work) // count)
        return [functools.partial(gram_of, work[k : k + size]) for k in range(0, len(work), size)]

    def gram_of(work):
        parts = [acc[k] for k in range(26)]
        for tile, i in work:
            rows = slice(i * 8, i * 8 + 8)
            if isinstance(tile, tuple):
                m = [jnp.where(lane >= HALF, matched[b, tile[0], rows], matched[b, tile[1], rows]) for b in range(BASIS)]
                d = jnp.where(lane >= HALF, sci[tile[0], rows], sci[tile[1], rows])
            else:
                m = [matched[b, tile, rows] for b in range(BASIS)]
                d = sci[tile, rows]
            k = 0
            for b in range(BASIS):
                for c in range(b, BASIS):
                    parts[k] = parts[k] + m[b] * m[c]
                    k += 1
            for b in range(BASIS):
                parts[15 + b] = parts[15 + b] + m[b]
                parts[20 + b] = parts[20 + b] + m[b] * d
            parts[25] = parts[25] + d
        for k in range(26):
            acc[k] = parts[k]

    rows_of((1, 2))

    def pair(p, carry):
        rows_of((2 * p + 1, 2 * p + 2), gram((2 * p - 1, 2 * p)))
        return carry

    lax.fori_loop(1, PAIRS, pair, 0)
    rows_of((0, TILES - 1), gram((TILES - 4, TILES - 3)))
    rows_of((TILES - 2,), gram(((0, TILES - 1),)))
    for step in gram((TILES - 2,), 1):
        step()
    rows = [jnp.sum(acc[k], axis=0, keepdims=True) for k in range(26)]
    rows = jnp.concatenate(rows + [jnp.zeros((NSUMS - 26, LANES), f32)], 0)
    total = jnp.broadcast_to(jnp.sum(rows, axis=1, keepdims=True), (NSUMS, LANES))
    packed = total[:8]
    for q in range(1, 4):
        packed = jnp.where(lane >= 32 * q, total[8 * q : 8 * q + 8], packed)
    for g in range(sums.shape[0]):
        sums[g] = packed


def solve(total, counted):
    def entry(k):
        return total[k : k + 1] / counted

    m, k = {}, 0
    for b in range(BASIS):
        for c in range(b, BASIS):
            m[b, c] = entry(k)
            k += 1
    for b in range(BASIS):
        m[b, BASIS] = entry(15 + b)
    m[BASIS, BASIS] = jnp.ones((1, LANES), f32)
    n = BASIS + 1
    for b in range(n):
        m[b, b] = m[b, b] + ridge
    rhs = [entry(20 + b) for b in range(BASIS)] + [entry(25)]
    inv = []
    for a in range(n):
        inv.append(1.0 / m[a, a])
        for b in range(a + 1, n):
            factor = m[a, b] * inv[a]
            for c in range(b, n):
                m[b, c] = m[b, c] - factor * m[a, c]
            rhs[b] = rhs[b] - factor * rhs[a]
    out = [None] * n
    for a in reversed(range(n)):
        value = rhs[a]
        for b in range(a + 1, n):
            value = value - m[a, b] * out[b]
        out[a] = value * inv[a]
    return out


def finish_kernel(counted, groups, sums, matched, sci, fcol_mat, frow_mat, diff, sig, coef, eh, el, keep, dout, sout, sems):
    packed = jnp.sum(sums[...], axis=0)
    spread = [jnp.broadcast_to(packed[:, 32 * q : 32 * q + 1], (8, LANES)) for q in range(4)]
    c = solve(jnp.concatenate(spread, 0), counted)
    lane = lax.broadcasted_iota(jnp.int32, (1, LANES), 1)
    coef_row = c[0]
    for b in range(1, BASIS + 1):
        coef_row = jnp.where(lane == b, c[b], coef_row)
    coef[...] = coef_row[:, : BASIS + 1]
    g = lax.axis_index(GRP[0]) * lax.axis_size(GRP[1]) + lax.axis_index(GRP[1])
    low_ok = jnp.where(g > 0, 1.0, 0.0).astype(f32)
    high_ok = jnp.where(g < groups - 1, 1.0, 0.0).astype(f32)

    def squares(d):
        return jnp.sum((d * d).reshape(ROWS // 8, 8, LANES), axis=0)

    def residual(t):
        total = c[0] * matched[0, t]
        for b in range(1, BASIS):
            total = total + c[b] * matched[b, t]
        d = sci[t] - total - c[BASIS]
        keep[t] = d
        return d

    def along_rows(ts, ds):
        halves = [split(d) for d in ds]
        d_hi = jnp.concatenate([x[0] for x in halves], 1)
        d_lo = jnp.concatenate([x[1] for x in halves], 1)
        for r in range(2):
            part = slice(0, FBAND) if r == 0 else slice(ROWS - FBAND, ROWS)
            rhs = jnp.concatenate([d_hi[part], d_hi[part], d_lo[part]], 0)
            e = jnp.dot(frow_mat[r * LANES : (r + 1) * LANES, :], rhs, preferred_element_type=f32)
            e_hi, e_lo = split(e)
            for s, t in enumerate(ts):
                eh[t, r * LANES : (r + 1) * LANES] = e_hi[:, s * LANES : (s + 1) * LANES]
                el[t, r * LANES : (r + 1) * LANES] = e_lo[:, s * LANES : (s + 1) * LANES]

    def emit(j):
        at = j * LANES if isinstance(j, int) else pl.multiple_of(j * LANES, LANES)
        dout[:, pl.ds(at, LANES)] = jnp.concatenate([keep[j][:, HALF:], keep[j + 1][:, :HALF]], 1)

    def send(source, target, first, end, sem):
        part = slice(first * LANES, end * LANES)
        copy = pltpu.make_async_copy(source.at[:, part], target.at[:, part], sems.at[sem])
        copy.start()
        return copy

    def pair(p, power):
        ts = (2 * p + 1, 2 * p + 2)
        ds = [residual(t) for t in ts]
        along_rows(ts, ds)
        emit(2 * p)
        emit(2 * p + 1)
        return power + squares(ds[0]) + squares(ds[1])

    low, high = residual(0), residual(TILES - 1)
    power = squares(jnp.where(lane >= HALF, low, high))
    low = low * jnp.where(lane >= HALF, 1.0, low_ok)
    high = high * jnp.where(lane < HALF, 1.0, high_ok)
    along_rows((0, TILES - 1), [low, high])
    middle = PAIRS // 2
    for p in range(middle):
        power = pair(p, power)
    copies = [send(dout, diff, 0, 2 * middle, 0)]
    for p in range(middle, PAIRS):
        power = pair(p, power)
    last = residual(TILES - 2)
    along_rows((TILES - 2,), [last])
    power = power + squares(last)
    emit(BLOCKS - 2)
    emit(BLOCKS - 1)
    copies.append(send(dout, diff, 2 * middle, BLOCKS, 1))
    noise = jnp.sum(jnp.sum(power, axis=0, keepdims=True), axis=1, keepdims=True) / float(ROWS * COLS)
    scale = 1.0 / jnp.sqrt(jnp.broadcast_to(noise, (1, LANES)) + epsilon)

    each = BLOCKS // PARTS
    for q in range(PARTS):
        for j in range(q * each, (q + 1) * each):
            e_hi = jnp.concatenate([eh[j], eh[j + 1]], 1)
            e_lo = jnp.concatenate([el[j], el[j + 1]], 1)
            s = jnp.dot(jnp.concatenate([e_hi, e_lo, e_hi], 1), fcol_mat[...], preferred_element_type=f32)
            sout[:, j * LANES : (j + 1) * LANES] = s * scale
        copies.append(send(sout, sig, q * each, (q + 1) * each, 2 + q))
    for copy in copies:
        copy.wait()


def call(kernel, ins, outs, scratch=(), mib=12, flops=0, nbytes=0, out_specs=None, **more):
    return pl.pallas_call(
        kernel,
        out_shape=outs,
        in_specs=ins,
        out_specs=jax.tree.map(lambda _: VMEM, outs) if out_specs is None else out_specs,
        scratch_shapes=list(scratch),
        compiler_params=params(mib),
        cost_estimate=pl.CostEstimate(flops=flops, bytes_accessed=nbytes, transcendentals=0),
        **more,
    )


def shape(*dims, dtype=f32):
    return jax.ShapeDtypeStruct(dims, dtype)


def ring(size):
    up = [(i, (i + 1) % size) for i in range(size)]
    return up, [(j, i) for i, j in up]


def shards(coadd, science, correlation, offset):
    groups = lax.axis_size(GRP)
    up, down = ring(groups)
    mats = [jnp.asarray(m) for m in (COL_MAT, ROW_MAT, FCOL_MAT, FROW_MAT)]
    to_left, to_right = call(edge_kernel, [VMEM] * 4, (shape(2 * EDGE, ROWS),) * 2)(
        coadd[:, :LANES], coadd[:, COLS - LANES :], science[:, :LANES], science[:, COLS - LANES :]
    )
    from_left = lax.ppermute(to_right, GRP, up)
    from_right = lax.ppermute(to_left, GRP, down)
    coadd, _, _ = lax.optimization_barrier((coadd, to_left, to_right))
    packed = call(pack_kernel, [SMEM, SMEM, VMEM], shape(BLOCKS, SENT, LANES), flops=1 << 20, nbytes=4 << 20)(
        correlation, offset, coadd
    )
    sent = call(functools.partial(patch_kernel, groups), [VMEM] * 3, shape(BLOCKS, SENT, LANES), input_output_aliases={0: 0})(
        packed, from_left, from_right
    )
    held = lax.all_to_all(sent, "visit", 0, 0, tiled=True)
    meta = held[:, ROWS + 4, :2].astype(jnp.int32)
    picked = call(
        pick_kernel,
        [SMEM, VMEM],
        shape(BLOCKS, WIN + 8, LANES),
        [pltpu.VMEM((STRIP + ROWS + 8, LANES), f32), pltpu.VMEM((8, STRIP + 2 * ROWS), f32)],
        nbytes=5 << 20,
    )(meta, held)
    win = lax.all_to_all(picked, "visit", 0, 0, tiled=True)
    tile16 = pltpu.VMEM((TILES + 1, WIN_PAD, LANES), bf16)
    matched, framed, sums = call(
        match_kernel,
        [VMEM] * 6,
        (shape(BASIS, TILES, ROWS, LANES), shape(TILES, ROWS, LANES), shape(groups, 8, LANES)),
        [tile16, tile16, pltpu.VMEM((26, 8, LANES), f32), pltpu.VMEM((LANES, 3 * LANES), f32)],
        flops=8 << 30,
        mib=24,
    )(win, science, from_left, from_right, *mats[:2])
    sums = lax.all_to_all(sums, GRP, 0, 0, tiled=True)
    block16 = pltpu.VMEM((TILES, ROWS, LANES), bf16)
    image = pltpu.VMEM((ROWS, COLS), f32)
    anywhere = pl.BlockSpec(memory_space=pl.ANY)
    return call(
        functools.partial(finish_kernel, float(ROWS * COLS * groups), groups),
        [VMEM] * 5,
        (shape(ROWS, COLS), shape(ROWS, COLS), shape(1, BASIS + 1)),
        [block16] * 2
        + [pltpu.VMEM((TILES, ROWS, LANES), f32), image, image, pltpu.SemaphoreType.DMA((2 + PARTS,))],
        flops=3 << 30,
        mib=30,
        out_specs=(anywhere, anywhere, VMEM),
    )(sums, matched, framed, *mats[2:])


def solution(mesh):
    split_mesh = Mesh(mesh.devices.reshape(mesh.shape["visit"], 4, 2), ("visit", "grp_0", "grp_1"))
    in_specs = (P("visit", GRP), P("visit", GRP), P("visit"), P("visit"))
    out_specs = (P("visit", GRP), P("visit", GRP), P("visit", None))
    return jax.shard_map(shards, mesh=split_mesh, in_specs=in_specs, out_specs=out_specs, check_vma=False)
```
